32 devices in a mesh: dp: 4 (over z), blk: 2 (over x), tensor: 4 (over y, core).
Axes of the slice: x: 2, y: 2, z: 4, core: 2. Of those that a mesh axis runs over, the one named last changes fastest.
Arguments:
- tokens: bfloat16 [4, 1024, 2048], P('dp', ('blk', 'tensor')), may hold values from -6 to 6
- doc_lengths: int32 [4, 3], P('dp'), may hold values from 1 to 768, as said below
- weight_qkv: bfloat16 [2048, 3, 2048], P(('dp', 'blk'), None, 'tensor'), may hold values from -0.125 to 0.125
- weight_out: bfloat16 [2048, 2048], P(('dp', 'blk'), 'tensor'), may hold values from -1 to 1
- weight_gate_up: bfloat16 [2048, 2, 8192], P(('dp', 'blk'), None, 'tensor'), may hold values from -0.125 to 0.125
- weight_down: bfloat16 [2048, 8192], P(('dp', 'blk'), 'tensor'), may hold values from -0.0625 to 0.0625
- norm_gains: float32 [2, 2048], P(None, ('dp', 'blk', 'tensor')), may hold values from 0.5 to 1.5
- cotangent: bfloat16 [4, 1024, 2048], P('dp', ('blk', 'tensor')), may hold values from -6 to 6
Outputs:
- block_output: bfloat16 [4, 1024, 2048], P('dp', ('blk', 'tensor'))
- input_grad: float32 [4, 1024, 2048], P('dp', ('blk', 'tensor'))
- grad_qkv: float32 [2048, 3, 2048], P(('dp', 'blk'), None, 'tensor')
- grad_out: float32 [2048, 2048], P(('dp', 'blk'), 'tensor')
- grad_gate_up: float32 [2048, 2, 8192], P(('dp', 'blk'), None, 'tensor')
- grad_down: float32 [2048, 8192], P(('dp', 'blk'), 'tensor')
- grad_gains: float32 [2, 2048], P(None, ('dp', 'blk', 'tensor'))
The draws below stay inside these ranges and needn't reach their ends.
Inputs may be any that keep to these rules, and one draw needn't show every extreme that they name: `doc_lengths`: each row holds 3 documents of one position or more, laid from the row's start; the positions after them are padding. One document of each row, which one drawn, is 1024 - 2 * (128) positions long; the others have at most 128 each, so that the long one starts within the row's first 512 positions and ends within its last 512.
All inputs are finite; a program needn't handle non-finite values.
Results may differ from the reference program's by a relative error of at most 0.02.
Values may be sent and summed in bfloat16 or wider, within the bound.
No kernel may reach another device: no remote copies, remote signals or barrier semaphores. Data moves between devices by JAX's collectives and lax.ppermute only.
A program may use at most 192 MiB of HBM per device.

```python
import math
import jax
import jax.numpy as jnp
from jax import lax

D = 2048
HEADS = 32
HEAD_DIM = 64
FF = 8192
TOK_BLK = 512
DOCS = 3
ROWS = 4
LEN = 1024


def draw_doc_lengths(key, part):
    key = jax.random.fold_in(key, 11)
    quarter = TOK_BLK // 4
    short_key, chosen_key = jax.random.split(key, 2)
    shorts = jax.random.randint(short_key, (ROWS, DOCS - 1), 1, quarter + 1).astype(jnp.int32)
    first_cell = (jnp.arange(ROWS, dtype=jnp.int32)[:, None] == 0) & (jnp.arange(DOCS - 1, dtype=jnp.int32)[None, :] == 0)
    shorts = jnp.where(first_cell, 1, shorts).astype(jnp.int32)
    longest = jnp.full((ROWS, 1), LEN - (DOCS - 1) * quarter, jnp.int32)
    chosen = jax.random.randint(chosen_key, (ROWS, 1), 0, DOCS).astype(jnp.int32)
    column = jnp.arange(DOCS, dtype=jnp.int32)[None, :]
    blank = jnp.zeros((ROWS, 1), jnp.int32)
    leading = jnp.concatenate([shorts, blank], axis=1)
    trailing = jnp.concatenate([blank, shorts], axis=1)
    return jnp.where(column < chosen, leading, jnp.where(column == chosen, longest, trailing)).astype(jnp.int32)


def shard_levels(rng, shape, cuts, smallest, largest):
    factor_of = 1.0
    for axis_at, blocks in cuts:
        steps = jax.random.uniform(jax.random.fold_in(jax.random.fold_in(rng, 6), axis_at), (blocks,), jnp.float32, smallest / len(cuts), largest / len(cuts))
        factor_of = factor_of * jnp.repeat(jnp.exp(steps), shape[axis_at] // blocks).reshape((-1,) + (1,) * (len(shape) - 1 - axis_at))
    return factor_of


def bell_draw(own_key, extent, deviation, most, cuts=(), kind=jnp.bfloat16):
    values = deviation * jax.random.normal(own_key, extent, jnp.float32)
    if cuts:
        values = values * shard_levels(own_key, extent, cuts, -0.22, 0.18)
    return jnp.clip(values, -most, most).astype(kind)


def setup_inputs(seed: int = 0) -> dict:
    keys = jax.random.split(jax.random.key(seed), 9)
    tokens = bell_draw(keys[0], (ROWS, LEN, D), 1.0, 6.0, ((0, 4), (1, 8)))
    doc_lengths = draw_doc_lengths(jax.random.fold_in(keys[8], 71), 0)
    weight_qkv = bell_draw(keys[2], (D, 3, D), D ** -0.5, 0.125, ((0, 8), (2, 4)))
    weight_out = bell_draw(keys[3], (D, D), (D // 64) ** -0.5, 1.0, ((0, 8), (1, 4)))
    weight_gate_up = bell_draw(keys[4], (D, 2, FF), D ** -0.5, 0.125, ((0, 8), (2, 4)))
    weight_down = bell_draw(keys[5], (D, FF), FF ** -0.5, 0.0625, ((0, 8), (1, 4)))
    norm_gains = jnp.clip(1.0 + 0.1 * jax.random.normal(keys[6], (2, D), jnp.float32), 0.5, 1.5)
    cotangent = bell_draw(keys[7], (ROWS, LEN, D), 1.0, 6.0, ((0, 4), (1, 8)))
    return {"tokens": tokens, "doc_lengths": doc_lengths, "weight_qkv": weight_qkv, "weight_out": weight_out, "weight_gate_up": weight_gate_up, "weight_down": weight_down, "norm_gains": norm_gains, "cotangent": cotangent}


EPSILON = 1e-05
ROPE_BASE = 130000.0
NEGATIVE = -1e+30
PRECISE = lax.Precision.HIGHEST

@jax.custom_vjp
def low(v):
    return lax.optimization_barrier(v.astype(jnp.bfloat16)).astype(jnp.float32)

@jax.custom_vjp
def low_back(v):
    return v

def low_keep(v):
    return (low(v), None)

def low_pass(kept, grad):
    return (grad,)

def back_keep(v):
    return (v, None)

def back_low(kept, grad):
    return (low(grad),)
low.defvjp(low_keep, low_pass)
low_back.defvjp(back_keep, back_low)

def layout(lengths, places):
    doc_ends = jnp.cumsum(lengths).astype(jnp.int32)
    passed = places[:, None] >= doc_ends[None, :]
    segment = lax.optimization_barrier(jnp.sum(passed.astype(jnp.int32), axis=1)).astype(jnp.int32)
    begins = lax.optimization_barrier(jnp.sum(jnp.where(passed, lengths[None, :], 0), axis=1)).astype(jnp.int32)
    return (segment, (places - begins).astype(jnp.int32))

def rope_tables(within, half_width):
    steps_up = jnp.arange(half_width, dtype=jnp.float32)
    frequency = ROPE_BASE ** (-2.0 * steps_up / (2 * half_width))
    angles = within.astype(jnp.float32)[:, None] * frequency[None, :]
    return (jnp.cos(angles), jnp.sin(angles))

def rotate(vectors, cosine_table, sine_table):
    half_width = vectors.shape[-1] // 2
    first_half = vectors[..., :half_width]
    second_half = vectors[..., half_width:]
    cosine_part = cosine_table[:, None, :]
    sine_part = sine_table[:, None, :]
    return jnp.concatenate([first_half * cosine_part - second_half * sine_part, second_half * cosine_part + first_half * sine_part], axis=-1)

def rms_unit(values):
    factor = lax.rsqrt(lax.optimization_barrier(jnp.mean(values * values, axis=-1, keepdims=True)) + EPSILON)
    return values * factor

def attend(queries, keys_all, values_all, segment, places):
    rows_block = math.gcd(LEN, 512)
    score_scale = HEAD_DIM ** (-0.5)

    def one_block(index_now):
        offset = (index_now * rows_block).astype(jnp.int32)
        block_queries = lax.dynamic_slice_in_dim(queries, offset, rows_block, 0)
        block_segment = lax.dynamic_slice_in_dim(segment, offset, rows_block, 0)
        block_places = lax.dynamic_slice_in_dim(places, offset, rows_block, 0)
        scores = low_back(jnp.einsum('qhd,khd->hqk', block_queries, keys_all, precision=PRECISE) * score_scale)
        allowed = (block_segment[:, None] == segment[None, :]) & (places[None, :] <= block_places[:, None])
        masked = jnp.where(allowed[None], scores, NEGATIVE)
        highest = lax.optimization_barrier(jnp.max(masked, axis=-1, keepdims=True))
        weights = jnp.where(allowed[None], jnp.exp(masked - highest), 0.0)
        weights = weights / lax.optimization_barrier(jnp.sum(weights, axis=-1, keepdims=True))
        return jnp.einsum('hqk,khd->qhd', weights, values_all, precision=PRECISE)
    blocks = lax.map(jax.checkpoint(one_block), jnp.arange(LEN // rows_block, dtype=jnp.int32))
    return blocks.reshape(LEN, HEADS, HEAD_DIM)

def forward(inputs, weight_qkv, weight_out, weight_gate_up, weight_down, norm_gains, segment, places, within):
    rows_all = inputs.shape[0]
    normed_first = low(rms_unit(inputs) * norm_gains[0])
    projected = low_back(jnp.einsum('td,dcf->tcf', normed_first, weight_qkv, precision=PRECISE))
    cosine_table, sine_table = rope_tables(within, HEAD_DIM // 2)
    shape_heads = (rows_all, HEADS, HEAD_DIM)
    queries = low(rotate(projected[:, 0].reshape(shape_heads), cosine_table, sine_table))
    keys_all = low(rotate(projected[:, 1].reshape(shape_heads), cosine_table, sine_table))
    values_all = low(projected[:, 2].reshape(shape_heads))
    present = (segment < DOCS).astype(jnp.float32)
    attended = attend(queries, keys_all, values_all, segment, places) * present[:, None, None]
    attended = low(low_back(attended.reshape(rows_all, D)))
    branch = low_back(jnp.dot(attended, weight_out.T, precision=PRECISE))
    middle = inputs + branch
    normed_second = low(rms_unit(middle) * norm_gains[1])
    gate_up = low_back(jnp.einsum('td,dcf->tcf', normed_second, weight_gate_up, precision=PRECISE))
    hidden = low(jax.nn.silu(gate_up[:, 0]) * gate_up[:, 1])
    feed_out = low_back(jnp.dot(hidden, weight_down.T, precision=PRECISE))
    return middle + feed_out

def reference(tokens, doc_lengths, weight_qkv, weight_out, weight_gate_up, weight_down, norm_gains, cotangent):
    places = jnp.arange(LEN, dtype=jnp.int32)

    def row_layout(lengths):
        return layout(lengths, places)
    segments, withins = jax.vmap(row_layout)(doc_lengths)

    def whole_layer(inputs, weight_qkv, weight_out, weight_gate_up, weight_down, norm_gains):

        def one_row(element):
            return forward(element[0], weight_qkv, weight_out, weight_gate_up, weight_down, norm_gains, element[1], places, element[2])
        return lax.map(one_row, (inputs, segments, withins))
    result, pullback = jax.vjp(whole_layer, tokens.astype(jnp.float32), weight_qkv.astype(jnp.float32), weight_out.astype(jnp.float32), weight_gate_up.astype(jnp.float32), weight_down.astype(jnp.float32), norm_gains)
    gradients = pullback(cotangent.astype(jnp.float32))
    return (result.astype(jnp.bfloat16), gradients[0], gradients[1], gradients[2], gradients[3], gradients[4], gradients[5])
```

```python
import functools

import jax
import jax.numpy as jnp
from jax import lax
from jax.experimental import pallas as pl
from jax.experimental.pallas import tpu as pltpu
from jax.sharding import PartitionSpec as P

HEAD_DIM = 64
PAIR = 2 * HEAD_DIM
EPSILON = 1e-05
ROPE_BASE = 130000.0
NEGATIVE = -1e30
QUERY_BLOCK = 256
UNROLLED = 4
LONG_ROW = 2048
PLANE = ("blk", "tensor")
F32 = jnp.float32
BF16 = jnp.bfloat16


def dot_nn(a, b):
    return lax.dot_general(a, b, (((1,), (0,)), ((), ())), preferred_element_type=F32)


def dot_nt(a, b):
    return lax.dot_general(a, b, (((1,), (1,)), ((), ())), preferred_element_type=F32)


def dot_tn(a, b):
    return lax.dot_general(a, b, (((0,), (0,)), ((), ())), preferred_element_type=F32)


def swap_by(value, axes, size, bits):
    return lax.ppermute(value, axes, [(i, i ^ bits) for i in range(size)])


def spread(rows, axes, size):
    near = jnp.concatenate(
        [rows] + [swap_by(rows, axes, size, bits) for bits in range(2, size, 2)], axis=0
    )
    return jnp.concatenate([near, swap_by(near, axes, size, 1)], axis=0)


def collect(left, right, product, axes, size):
    half = left.shape[0] // 2
    sent = product(left[half:], right).astype(BF16)
    received = swap_by(sent, axes, size, 1)
    near = (product(left[:half], right) + received.astype(F32)).astype(BF16)
    rows = near.shape[0] // (size // 2)
    total = near[:rows].astype(F32)
    for place in range(1, size // 2):
        block = near[place * rows : (place + 1) * rows]
        total = total + swap_by(block, axes, size, 2 * place).astype(F32)
    return total


def gather_small(value, axis_sizes):
    for axis, size in reversed(axis_sizes):
        index = lax.axis_index(axis)
        bit = 1
        while bit < size:
            other = swap_by(value, axis, size, bit)
            low = (index & bit) == 0
            value = jnp.concatenate(
                [jnp.where(low, value, other), jnp.where(low, other, value)], axis=1
            )
            bit *= 2
    return value


def scatter_small(value, axis_sizes):
    for axis, size in axis_sizes:
        index = lax.axis_index(axis)
        bit = size // 2
        while bit >= 1:
            half = value.shape[1] // 2
            low = (index & bit) == 0
            kept = jnp.where(low, value[:, :half], value[:, half:])
            sent = jnp.where(low, value[:, half:], value[:, :half])
            value = kept + swap_by(sent, axis, size, bit)
            bit //= 2
    return value


def gather_weight(weight, blocks):
    rows, kinds, columns = weight.shape
    own = columns // blocks
    parted = weight.reshape(rows, kinds, blocks, own).transpose(2, 0, 1, 3)
    parted = parted.reshape(blocks, rows, kinds * own)
    mixed = lax.all_to_all(parted, "blk", 0, 0, tiled=True).reshape(blocks * rows, kinds * own)
    return lax.all_gather(mixed, "dp", axis=0, tiled=True)


def scatter_weight(grads, blocks, kinds):
    own = grads.shape[1] // kinds
    summed = lax.psum_scatter(grads.astype(BF16), "dp", scatter_dimension=0, tiled=True)
    rows = summed.shape[0] // blocks
    parted = lax.all_to_all(
        summed.reshape(blocks, rows, kinds * own), "blk", 0, 0, tiled=True
    )
    parted = parted.reshape(blocks, rows, kinds, own).transpose(1, 2, 0, 3)
    return parted.reshape(rows, kinds, blocks * own).astype(F32)


def swap_halves(values):
    lane = lax.broadcasted_iota(jnp.int32, values.shape, 1)
    half = HEAD_DIM // 2
    return jnp.where(
        lane % HEAD_DIM < half,
        pltpu.roll(values, PAIR - half, 1),
        pltpu.roll(values, half, 1),
    )


def relative_place(block, info_ref, blocks, rows):
    bits = lax.bitwise_xor(jnp.int32(block), info_ref[0])
    place = lax.shift_right_logical(bits, 1) + (bits & 1) * (blocks // 2)
    return pl.ds(pl.multiple_of(place * rows, rows), rows)


def document_start(places, info_ref):
    end_0 = info_ref[1]
    end_1 = info_ref[2]
    end_2 = info_ref[3]
    start = jnp.where(places >= end_0, end_0, 0)
    start = jnp.where(places >= end_1, end_1, start)
    return jnp.where(places >= end_2, end_2, start)


def head_lanes(shape, head):
    lane = lax.broadcasted_iota(jnp.int32, shape, 1)
    return (lane < HEAD_DIM) if head == 0 else (lane >= HEAD_DIM)


def only_head(values, head):
    return jnp.where(head_lanes(values.shape, head), values, jnp.zeros_like(values))


def attend_kernel(
    blocks,
    info_ref,
    q_ref,
    k_ref,
    v_ref,
    cos_ref,
    sin_ref,
    out_ref,
    q_row,
    k_row,
    v_row,
    log_ref,
):
    length = q_ref.shape[0]
    rows = length // blocks
    score_scale = HEAD_DIM ** (-0.5)
    for block in range(blocks):
        here = relative_place(block, info_ref, blocks, rows)
        there = pl.ds(block * rows, rows)
        cosine, sine = cos_ref[here, :], sin_ref[here, :]
        q, k = q_ref[here, :], k_ref[here, :]
        q_row[there, :] = ((q * cosine + swap_halves(q) * sine) * score_scale).astype(BF16)
        k_row[there, :] = (k * cosine + swap_halves(k) * sine).astype(BF16)
        v_row[there, :] = v_ref[here, :].astype(BF16)

    tall = max(QUERY_BLOCK, rows)

    def query_step(first, width):
        queries = q_row[pl.ds(first, tall), :]
        places = first + lax.broadcasted_iota(jnp.int32, (tall, 1), 0)
        keys_at = lax.broadcasted_iota(jnp.int32, (tall, width), 1)
        allowed = (keys_at <= places) & (keys_at >= document_start(places, info_ref))
        results = []
        logs = []
        for head in range(2):
            scores = dot_nt(only_head(queries, head), k_row[:width, :])
            scores = jnp.where(allowed, scores, NEGATIVE)
            highest = jnp.max(scores, axis=1, keepdims=True)
            weights = jnp.exp(scores - highest)
            total = jnp.sum(weights, axis=1, keepdims=True)
            results.append(dot_nn(weights.astype(BF16), v_row[:width, :]) / total)
            logs.append(highest + jnp.log(total))
        first_head = head_lanes((tall, PAIR), 0)
        present = (places < info_ref[3]).astype(F32)
        merged = (jnp.where(first_head, results[0], results[1]) * present).astype(BF16)
        log_ref[pl.ds(first, tall), :] = jnp.where(first_head, logs[0], logs[1])
        return merged

    def put(merged, first_block):
        for part in range(tall // rows):
            here = relative_place(first_block + part, info_ref, blocks, rows)
            out_ref[here, :] = merged[part * rows : (part + 1) * rows]

    steps = length // tall
    if steps <= UNROLLED:
        for step in range(steps):
            put(query_step(step * tall, (step + 1) * tall), step * (tall // rows))
    else:

        @pl.loop(0, steps)
        def _(step):
            put(query_step(pl.multiple_of(step * tall, tall), length), step * (tall // rows))


def attend(info, projected, cosine, sine, blocks):
    length, width = projected.shape
    pairs = width // 3 // PAIR
    whole = lambda kind: pl.BlockSpec((length, PAIR), lambda p, _: (0, kind * pairs + p))
    table = pl.BlockSpec((length, PAIR), lambda p, _: (0, 0))
    shape = lambda kind: jax.ShapeDtypeStruct((length, pairs * PAIR), kind)
    return pl.pallas_call(
        functools.partial(attend_kernel, blocks),
        grid_spec=pltpu.PrefetchScalarGridSpec(
            num_scalar_prefetch=1,
            grid=(pairs,),
            in_specs=[whole(0), whole(1), whole(2), table, table],
            out_specs=[whole(0)] * 5,
        ),
        out_shape=[shape(BF16), shape(BF16), shape(BF16), shape(BF16), shape(F32)],
        compiler_params=pltpu.CompilerParams(vmem_limit_bytes=48 * 2**20),
        cost_estimate=pl.CostEstimate(
            flops=8 * pairs * length * length * PAIR // 2,
            bytes_accessed=6 * length * width,
            transcendentals=pairs * length * length,
        ),
        name="attend",
    )(info, projected, projected, projected, cosine, sine)


def attend_back_kernel(
    blocks,
    info_ref,
    q_row,
    k_row,
    v_row,
    log_ref,
    out_ref,
    grad_ref,
    cos_ref,
    sin_ref,
    back_ref,
    g_row,
    q_sum,
    k_sum,
    v_sum,
    log_flat,
    inner_flat,
):
    length = q_row.shape[0]
    rows = length // blocks
    score_scale = HEAD_DIM ** (-0.5)
    kind = pl.program_id(1)
    tall = max(QUERY_BLOCK, rows)

    @pl.when(kind == 0)
    def _():
        for block in range(blocks):
            here = relative_place(block, info_ref, blocks, rows)
            there = pl.ds(block * rows, rows)
            places = block * rows + lax.broadcasted_iota(jnp.int32, (rows, 1), 0)
            present = (places < info_ref[3]).astype(F32)
            grads = grad_ref[here, :].astype(F32) * present
            g_row[there, :] = grads.astype(BF16)
            inner = (grads * out_ref[here, :].astype(F32)).T
            for head in range(2):
                span = slice(head * HEAD_DIM, (head + 1) * HEAD_DIM)
                inner_flat[head : head + 1, there] = jnp.sum(inner[span], axis=0, keepdims=True)
            logs = log_ref[there, :].T
            for head in range(2):
                log_flat[head : head + 1, there] = logs[head * HEAD_DIM : head * HEAD_DIM + 1]
        q_sum[...] = jnp.zeros_like(q_sum)

        def key_step(first, from_query):
            width = length - from_query
            span = slice(from_query, length)
            keys = k_row[pl.ds(first, tall), :]
            values = v_row[pl.ds(first, tall), :]
            keys_at = first + lax.broadcasted_iota(jnp.int32, (tall, 1), 0)
            places = from_query + lax.broadcasted_iota(jnp.int32, (1, width), 1)
            allowed = (keys_at <= places) & (keys_at >= document_start(places, info_ref))
            queries, grads = q_row[span, :], g_row[span, :]
            k_parts = []
            v_parts = []
            for head in range(2):
                keys_head = only_head(keys, head)
                scores = dot_nt(keys_head, queries)
                raised = jnp.exp(scores - log_flat[head : head + 1, span])
                weights = jnp.where(allowed, raised, 0.0)
                grad_weights = dot_nt(only_head(values, head), grads)
                grad_scores = weights * (grad_weights - inner_flat[head : head + 1, span])
                grad_scores = grad_scores.astype(BF16)
                v_parts.append(dot_nn(weights.astype(BF16), grads))
                k_parts.append(dot_nn(grad_scores, queries))
                q_sum[span, :] += dot_tn(grad_scores, keys_head)
            first_head = head_lanes((tall, PAIR), 0)
            k_sum[pl.ds(first, tall), :] = jnp.where(first_head, k_parts[0], k_parts[1])
            v_sum[pl.ds(first, tall), :] = jnp.where(first_head, v_parts[0], v_parts[1])

        steps = length // tall
        if steps <= UNROLLED:
            for step in range(steps):
                key_step(step * tall, step * tall)
        else:

            @pl.loop(0, steps)
            def _(step):
                key_step(pl.multiple_of(step * tall, tall), 0)

    def give(source, turned, scale):
        for block in range(blocks):
            here = relative_place(block, info_ref, blocks, rows)
            grads = source[pl.ds(block * rows, rows), :] * scale
            if turned:
                grads = grads * cos_ref[here, :] - swap_halves(grads) * sin_ref[here, :]
            back_ref[here, :] = grads.astype(BF16)

    pl.when(kind == 0)(lambda: give(q_sum, True, score_scale))
    pl.when(kind == 1)(lambda: give(k_sum, True, 1.0))
    pl.when(kind == 2)(lambda: give(v_sum, False, 1.0))


def attend_back(info, q_row, k_row, v_row, logs, attended, grads, cosine, sine, blocks):
    length, width = q_row.shape
    pairs = width // PAIR
    one = pl.BlockSpec((length, PAIR), lambda p, c, _: (0, p))
    table = pl.BlockSpec((length, PAIR), lambda p, c, _: (0, 0))
    return pl.pallas_call(
        functools.partial(attend_back_kernel, blocks),
        grid_spec=pltpu.PrefetchScalarGridSpec(
            num_scalar_prefetch=1,
            grid=(pairs, 3),
            in_specs=[one] * 6 + [table] * 2,
            out_specs=pl.BlockSpec((length, PAIR), lambda p, c, _: (0, c * pairs + p)),
            scratch_shapes=[
                pltpu.VMEM((length, PAIR), BF16),
                pltpu.VMEM((length, PAIR), F32),
                pltpu.VMEM((length, PAIR), F32),
                pltpu.VMEM((length, PAIR), F32),
                pltpu.VMEM((8, length), F32),
                pltpu.VMEM((8, length), F32),
            ],
        ),
        out_shape=jax.ShapeDtypeStruct((length, 3 * width), BF16),
        compiler_params=pltpu.CompilerParams(vmem_limit_bytes=48 * 2**20),
        cost_estimate=pl.CostEstimate(
            flops=20 * pairs * length * length * PAIR // 2,
            bytes_accessed=20 * length * width,
            transcendentals=pairs * length * length,
        ),
        name="attend_back",
    )(info, q_row, k_row, v_row, logs, attended, grads, cosine, sine)


def whole_pairs(values, kinds):
    own = values.shape[1] // kinds
    if own % PAIR == 0:
        return values
    values = jnp.pad(values.reshape(-1, kinds, own), ((0, 0), (0, 0), (0, PAIR - own % PAIR)))
    return values.reshape(values.shape[0], -1)


def own_heads(values, kinds, own):
    return values.reshape(values.shape[0], kinds, -1)[:, :, :own].reshape(values.shape[0], -1)


def rms_unit(values):
    factor = lax.rsqrt(jnp.mean(values * values, axis=-1, keepdims=True) + EPSILON)
    return (values * factor, factor)


def norm_back(grad_normed, unit_rows, factor, gain_row):
    scaled_grad = grad_normed * gain_row
    inner_mean = jnp.mean(scaled_grad * unit_rows, axis=-1, keepdims=True)
    return (
        factor * (scaled_grad - unit_rows * inner_mean),
        jnp.sum(grad_normed * unit_rows, axis=0),
    )


def row_layout(lengths, places):
    ends = [jnp.sum(lengths[: i + 1]) for i in range(lengths.shape[0])]
    begins = jnp.zeros_like(places)
    for end in ends:
        begins = jnp.where(places >= end, end, begins)
    return ends, places - begins


def rope_tables(within):
    half = HEAD_DIM // 2
    steps_up = jnp.arange(half, dtype=F32)
    frequency = ROPE_BASE ** (-2.0 * steps_up / HEAD_DIM)
    angles = within.astype(F32)[:, None] * frequency[None, :]
    cosine, sine = jnp.cos(angles), jnp.sin(angles)
    return (
        jnp.concatenate([cosine] * 4, axis=1),
        jnp.concatenate([-sine, sine, -sine, sine], axis=1),
    )


def body(
    tokens, doc_lengths, weight_qkv, weight_out, weight_gate_up, weight_down, norm_gains, cotangent
):
    sizes = [(axis, lax.axis_size(axis)) for axis in ("dp", "blk", "tensor")]
    (_, _), (_, size_blk), (_, size_tensor) = sizes
    group = size_blk * size_tensor
    local_rows = tokens.shape[1]
    lengths = doc_lengths[0]

    me = (lax.axis_index("blk") * size_tensor + lax.axis_index("tensor")).astype(jnp.int32)
    order = jnp.array([*range(0, group, 2), *range(1, group, 2)], jnp.int32)
    places = (lax.bitwise_xor(order, me)[:, None] * local_rows) + jnp.arange(
        local_rows, dtype=jnp.int32
    )[None, :]
    ends, within = row_layout(lengths, places.reshape(-1))
    info = jnp.stack([me] + ends).astype(jnp.int32)
    cosine, sine = rope_tables(within)

    full_qkv = gather_weight(weight_qkv, size_blk)
    full_out = gather_weight(weight_out[:, None, :], size_blk)
    full_gate_up = gather_weight(weight_gate_up, size_blk)
    full_down = gather_weight(weight_down[:, None, :], size_blk)
    gain_pair = gather_small(norm_gains, sizes)
    gain_first, gain_second = gain_pair[0], gain_pair[1]

    inputs = tokens[0].astype(F32)
    unit_first, factor_first = rms_unit(inputs)
    normed_first = spread((unit_first * gain_first).astype(BF16), PLANE, group)
    projected = dot_nn(normed_first, full_qkv)
    features = full_out.shape[1]
    attended, q_row, k_row, v_row, logs = attend(
        info, whole_pairs(projected, 3), cosine, sine, group
    )
    attended_here = own_heads(attended, 1, features)
    branch = collect(attended_here, full_out, dot_nt, PLANE, group)
    middle = inputs + branch
    unit_second, factor_second = rms_unit(middle)
    normed_second = spread((unit_second * gain_second).astype(BF16), PLANE, group)
    hidden_here = full_gate_up.shape[1] // 2
    gate = dot_nn(normed_second, full_gate_up[:, :hidden_here])
    up = dot_nn(normed_second, full_gate_up[:, hidden_here:])
    sigmoid_gate = jax.nn.sigmoid(gate)
    activated = gate * sigmoid_gate
    hidden = (activated * up).astype(BF16)
    feed_out = collect(hidden, full_down, dot_nt, PLANE, group)
    grad_output = cotangent[0].astype(F32)
    last_rows = cotangent[0]
    if normed_second.shape[0] > LONG_ROW:
        last_rows, feed_out = lax.optimization_barrier((last_rows, feed_out))
    grad_feed = spread(last_rows, PLANE, group)
    outcome = (middle + feed_out).astype(BF16)
    grad_down = dot_tn(grad_feed, hidden)
    grad_hidden = dot_nn(grad_feed, full_down)
    silu_slope = sigmoid_gate * (1.0 + gate * (1.0 - sigmoid_gate))
    grad_gates = jnp.concatenate(
        [
            (grad_hidden * up * silu_slope).astype(BF16),
            (grad_hidden * activated).astype(BF16),
        ],
        axis=1,
    )
    grad_gate_up = dot_tn(normed_second, grad_gates)
    grad_normed_second = collect(grad_gates, full_gate_up, dot_nt, PLANE, group)
    grad_middle_norm, sum_second = norm_back(
        grad_normed_second, unit_second, factor_second, gain_second
    )
    grad_middle = grad_output + grad_middle_norm
    grad_branch = spread(grad_middle.astype(BF16), PLANE, group)
    grad_out = dot_tn(grad_branch, attended_here)
    grad_attended = dot_nn(grad_branch, full_out).astype(BF16)
    grad_projected = attend_back(
        info,
        q_row,
        k_row,
        v_row,
        logs,
        attended,
        whole_pairs(grad_attended, 1),
        cosine,
        sine,
        group,
    )
    grad_projected = own_heads(grad_projected, 3, features)
    grad_qkv = dot_tn(normed_first, grad_projected)
    grad_normed_first = collect(grad_projected, full_qkv, dot_nt, PLANE, group)
    grad_input_norm, sum_first = norm_back(grad_normed_first, unit_first, factor_first, gain_first)
    grad_input = grad_middle + grad_input_norm

    total_down = scatter_weight(grad_down, size_blk, 1)[:, 0]
    total_gate_up = scatter_weight(grad_gate_up, size_blk, 2)
    total_out = scatter_weight(grad_out, size_blk, 1)[:, 0]
    total_qkv = scatter_weight(grad_qkv, size_blk, 3)
    gain_sums = scatter_small(jnp.stack([sum_first, sum_second]), sizes)
    return (
        outcome[None],
        grad_input[None],
        total_qkv,
        total_out,
        total_gate_up,
        total_down,
        gain_sums,
    )


def solution(mesh):
    return jax.shard_map(
        body,
        mesh=mesh,
        in_specs=(
            P("dp", ("blk", "tensor"), None),
            P("dp", None),
            P(("dp", "blk"), None, "tensor"),
            P(("dp", "blk"), "tensor"),
            P(("dp", "blk"), None, "tensor"),
            P(("dp", "blk"), "tensor"),
            P(None, ("dp", "blk", "tensor")),
            P("dp", ("blk", "tensor"), None),
        ),
        out_specs=(
            P("dp", ("blk", "tensor"), None),
            P("dp", ("blk", "tensor"), None),
            P(("dp", "blk"), None, "tensor"),
            P(("dp", "blk"), "tensor"),
            P(("dp", "blk"), None, "tensor"),
            P(("dp", "blk"), "tensor"),
            P(None, ("dp", "blk", "tensor")),
        ),
        check_vma=False,
    )
```

```python
import functools

import jax
import jax.numpy as jnp
from jax import lax
from jax.experimental import pallas as pl
from jax.experimental.pallas import tpu as pltpu
from jax.sharding import PartitionSpec as P

HEAD_DIM = 64
PAIR = 2 * HEAD_DIM
EPSILON = 1e-05
ROPE_BASE = 130000.0
NEGATIVE = -1e30
QUERY_BLOCK = 256
UNROLLED = 4
LONG_ROW = 2048
PLANE = ("blk", "tensor")
F32 = jnp.float32
BF16 = jnp.bfloat16


def dot_nn(a, b):
    return lax.dot_general(a, b, (((1,), (0,)), ((), ())), preferred_element_type=F32)


def dot_nt(a, b):
    return lax.dot_general(a, b, (((1,), (1,)), ((), ())), preferred_element_type=F32)


def dot_tn(a, b):
    return lax.dot_general(a, b, (((0,), (0,)), ((), ())), preferred_element_type=F32)


def named(name, function, *args):
    with jax.named_scope(name):
        return function(*args)


def after(value, *events):
    return lax.optimization_barrier((value, *events))[0]


def together(*values):
    return lax.optimization_barrier(values)


def swap_by(value, axes, size, bits):
    return lax.ppermute(value, axes, [(i, i ^ bits) for i in range(size)])


def join_kernel(steps, near_ref, far_ref, out_ref):
    step = pl.program_id(0)

    @pl.when(step < steps)
    def _():
        out_ref[...] = near_ref[...]

    @pl.when(step >= steps)
    def _():
        out_ref[...] = far_ref[...]


def join_halves(near, far):
    rows, width = near.shape
    steps = max(1, rows // 128)
    block = (rows // steps, width)
    return pl.pallas_call(
        functools.partial(join_kernel, steps),
        grid=(2 * steps,),
        in_specs=[
            pl.BlockSpec(block, lambda i: (jnp.minimum(i, steps - 1), 0)),
            pl.BlockSpec(block, lambda i: (jnp.maximum(i - steps, 0), 0)),
        ],
        out_specs=pl.BlockSpec(block, lambda i: (i, 0)),
        out_shape=jax.ShapeDtypeStruct((2 * rows, width), near.dtype),
        cost_estimate=pl.CostEstimate(
            flops=0, bytes_accessed=8 * rows * width, transcendentals=0
        ),
        name="join_halves",
    )(near, far)


def spread(rows, axes, size):
    near = jnp.concatenate(
        [rows] + [swap_by(rows, axes, size, bits) for bits in range(2, size, 2)], axis=0
    )
    return join_halves(near, swap_by(near, axes, size, 1))


def collect(left, right, product, axes, size, *tied, begin=()):
    half = left.shape[0] // 2
    received = swap_by(product(left[half:], right).astype(BF16), axes, size, 1)
    near = (product(left[:half], right) + received.astype(F32)).astype(BF16)
    if tied:
        near, *tied = together(near, *tied)
    if begin:
        near = after(near, *begin)
    rows = near.shape[0] // (size // 2)
    blocks = [
        swap_by(near[place * rows : (place + 1) * rows], axes, size, 2 * place)
        for place in range(1, size // 2)
    ]
    summed = sum([block.astype(F32) for block in blocks], near[:rows].astype(F32))
    return summed, blocks[0], *tied


def gather_small(value, axis_sizes):
    for axis, size in reversed(axis_sizes):
        index = lax.axis_index(axis)
        bit = 1
        while bit < size:
            other = swap_by(value, axis, size, bit)
            low = (index & bit) == 0
            value = jnp.concatenate(
                [jnp.where(low, value, other), jnp.where(low, other, value)], axis=1
            )
            bit *= 2
    return value


def scatter_small(value, axis_sizes):
    sizes = [size for _, size in axis_sizes]
    kinds = value.shape[0]
    value = value.reshape(kinds, sizes[0], -1).swapaxes(1, 2).reshape(kinds, *sizes[1:], -1)
    value = value.reshape(kinds, -1, value.shape[-1] // sizes[0], sizes[0])
    value = value.swapaxes(2, 3).reshape(kinds, -1)
    for axis, size in (*axis_sizes[1:], axis_sizes[0]):
        index = lax.axis_index(axis)
        bit = size // 2
        while bit >= 1:
            half = value.shape[1] // 2
            low = (index & bit) == 0
            kept = jnp.where(low, value[:, :half], value[:, half:])
            sent = jnp.where(low, value[:, half:], value[:, :half])
            value = kept + swap_by(sent, axis, size, bit)
            bit //= 2
    return value


def trade(blocks, axis):
    return lax.all_to_all(blocks, axis, 0, 0, tiled=True)


def split_columns(weight, blocks):
    rows, kinds, columns = weight.shape
    parted = weight.reshape(rows, kinds, blocks, columns // blocks).transpose(2, 0, 1, 3)
    return parted.reshape(blocks, rows, -1)


def swap_columns(weights, blocks):
    parts = [split_columns(weight, blocks) for weight in weights]
    traded = trade(jnp.concatenate(parts, axis=2), "blk")
    traded = traded.reshape(-1, traded.shape[2])
    cuts = []
    start = 0
    for part in parts:
        cuts.append(traded[:, start : start + part.shape[2]])
        start += part.shape[2]
    return cuts


def gather_rows(weight, *events):
    return lax.all_gather(after(weight, *events), "dp", axis=0, tiled=True)


def sum_rows(grads):
    return lax.psum_scatter(grads, "dp", scatter_dimension=0, tiled=True)


def return_columns(summed, blocks, kinds, own):
    parted = trade(summed.reshape(blocks, -1, summed.shape[1]), "blk").astype(F32)
    totals = []
    start = 0
    for kind in kinds:
        columns = [
            [parted[b, :, start + i * own : start + (i + 1) * own] for b in range(blocks)]
            for i in range(kind)
        ]
        totals.append(jnp.stack([jnp.concatenate(part, axis=1) for part in columns], axis=1))
        start += kind * own
    return totals


def swap_halves(values):
    lane = lax.broadcasted_iota(jnp.int32, values.shape, 1)
    half = HEAD_DIM // 2
    return jnp.where(
        lane % HEAD_DIM < half,
        pltpu.roll(values, PAIR - half, 1),
        pltpu.roll(values, half, 1),
    )


def relative_place(block, info_ref, blocks, rows):
    bits = lax.bitwise_xor(jnp.int32(block), info_ref[0])
    place = lax.shift_right_logical(bits, 1) + (bits & 1) * (blocks // 2)
    return pl.ds(pl.multiple_of(place * rows, rows), rows)


def document_start(places, info_ref):
    end_0 = info_ref[1]
    end_1 = info_ref[2]
    end_2 = info_ref[3]
    start = jnp.where(places >= end_0, end_0, 0)
    start = jnp.where(places >= end_1, end_1, start)
    return jnp.where(places >= end_2, end_2, start)


def head_lanes(shape, head):
    lane = lax.broadcasted_iota(jnp.int32, shape, 1)
    return (lane < HEAD_DIM) if head == 0 else (lane >= HEAD_DIM)


def only_head(values, head):
    return jnp.where(head_lanes(values.shape, head), values, jnp.zeros_like(values))


def attend_kernel(
    blocks,
    info_ref,
    q_ref,
    k_ref,
    v_ref,
    cos_ref,
    sin_ref,
    out_ref,
    q_row,
    k_row,
    v_row,
    log_ref,
):
    length = q_ref.shape[0]
    rows = length // blocks
    score_scale = HEAD_DIM ** (-0.5)
    for block in range(blocks):
        here = relative_place(block, info_ref, blocks, rows)
        there = pl.ds(block * rows, rows)
        cosine, sine = cos_ref[here, :], sin_ref[here, :]
        q, k = q_ref[here, :], k_ref[here, :]
        q_row[there, :] = ((q * cosine + swap_halves(q) * sine) * score_scale).astype(BF16)
        k_row[there, :] = (k * cosine + swap_halves(k) * sine).astype(BF16)
        v_row[there, :] = v_ref[here, :].astype(BF16)

    tall = max(QUERY_BLOCK, rows)

    def query_step(first, width):
        queries = q_row[pl.ds(first, tall), :]
        places = first + lax.broadcasted_iota(jnp.int32, (tall, 1), 0)
        keys_at = lax.broadcasted_iota(jnp.int32, (tall, width), 1)
        allowed = (keys_at <= places) & (keys_at >= document_start(places, info_ref))
        results = []
        logs = []
        for head in range(2):
            scores = dot_nt(only_head(queries, head), k_row[:width, :])
            scores = jnp.where(allowed, scores, NEGATIVE)
            highest = jnp.max(scores, axis=1, keepdims=True)
            weights = jnp.exp(scores - highest)
            total = jnp.sum(weights, axis=1, keepdims=True)
            results.append(dot_nn(weights.astype(BF16), v_row[:width, :]) / total)
            logs.append(highest + jnp.log(total))
        first_head = head_lanes((tall, PAIR), 0)
        present = (places < info_ref[3]).astype(F32)
        merged = (jnp.where(first_head, results[0], results[1]) * present).astype(BF16)
        log_ref[pl.ds(first, tall), :] = jnp.where(first_head, logs[0], logs[1])
        return merged

    def put(merged, first_block):
        for part in range(tall // rows):
            here = relative_place(first_block + part, info_ref, blocks, rows)
            out_ref[here, :] = merged[part * rows : (part + 1) * rows]

    steps = length // tall
    if steps <= UNROLLED:
        for step in range(steps):
            put(query_step(step * tall, (step + 1) * tall), step * (tall // rows))
    else:

        @pl.loop(0, steps)
        def _(step):
            put(query_step(pl.multiple_of(step * tall, tall), length), step * (tall // rows))


def attend(info, projected, cosine, sine, blocks):
    length, width = projected.shape
    pairs = width // 3 // PAIR
    whole = lambda kind: pl.BlockSpec((length, PAIR), lambda p, _: (0, kind * pairs + p))
    table = pl.BlockSpec((length, PAIR), lambda p, _: (0, 0))
    shape = lambda kind: jax.ShapeDtypeStruct((length, pairs * PAIR), kind)
    return pl.pallas_call(
        functools.partial(attend_kernel, blocks),
        grid_spec=pltpu.PrefetchScalarGridSpec(
            num_scalar_prefetch=1,
            grid=(pairs,),
            in_specs=[whole(0), whole(1), whole(2), table, table],
            out_specs=[whole(0)] * 5,
        ),
        out_shape=[shape(BF16), shape(BF16), shape(BF16), shape(BF16), shape(F32)],
        compiler_params=pltpu.CompilerParams(vmem_limit_bytes=48 * 2**20),
        cost_estimate=pl.CostEstimate(
            flops=8 * pairs * length * length * PAIR // 2,
            bytes_accessed=6 * length * width,
            transcendentals=pairs * length * length,
        ),
        name="attend",
    )(info, projected, projected, projected, cosine, sine)


def attend_back_kernel(
    blocks,
    info_ref,
    q_row,
    k_row,
    v_row,
    log_ref,
    out_ref,
    grad_ref,
    cos_ref,
    sin_ref,
    back_ref,
    g_row,
    q_sum,
    k_sum,
    v_sum,
    log_flat,
    inner_flat,
):
    length = q_row.shape[0]
    rows = length // blocks
    score_scale = HEAD_DIM ** (-0.5)
    kind = pl.program_id(1)
    tall = max(QUERY_BLOCK, rows)

    @pl.when(kind == 0)
    def _():
        for block in range(blocks):
            here = relative_place(block, info_ref, blocks, rows)
            there = pl.ds(block * rows, rows)
            places = block * rows + lax.broadcasted_iota(jnp.int32, (rows, 1), 0)
            present = (places < info_ref[3]).astype(F32)
            grads = grad_ref[here, :].astype(F32) * present
            g_row[there, :] = grads.astype(BF16)
            inner = (grads * out_ref[here, :].astype(F32)).T
            for head in range(2):
                span = slice(head * HEAD_DIM, (head + 1) * HEAD_DIM)
                inner_flat[head : head + 1, there] = jnp.sum(inner[span], axis=0, keepdims=True)
            logs = log_ref[there, :].T
            for head in range(2):
                log_flat[head : head + 1, there] = logs[head * HEAD_DIM : head * HEAD_DIM + 1]
        q_sum[...] = jnp.zeros_like(q_sum)

        def key_step(first, from_query):
            width = length - from_query
            span = slice(from_query, length)
            keys = k_row[pl.ds(first, tall), :]
            values = v_row[pl.ds(first, tall), :]
            keys_at = first + lax.broadcasted_iota(jnp.int32, (tall, 1), 0)
            places = from_query + lax.broadcasted_iota(jnp.int32, (1, width), 1)
            allowed = (keys_at <= places) & (keys_at >= document_start(places, info_ref))
            queries, grads = q_row[span, :], g_row[span, :]
            k_parts = []
            v_parts = []
            for head in range(2):
                keys_head = only_head(keys, head)
                scores = dot_nt(keys_head, queries)
                raised = jnp.exp(scores - log_flat[head : head + 1, span])
                weights = jnp.where(allowed, raised, 0.0)
                grad_weights = dot_nt(only_head(values, head), grads)
                grad_scores = weights * (grad_weights - inner_flat[head : head + 1, span])
                grad_scores = grad_scores.astype(BF16)
                v_parts.append(dot_nn(weights.astype(BF16), grads))
                k_parts.append(dot_nn(grad_scores, queries))
                q_sum[span, :] += dot_tn(grad_scores, keys_head)
            first_head = head_lanes((tall, PAIR), 0)
            k_sum[pl.ds(first, tall), :] = jnp.where(first_head, k_parts[0], k_parts[1])
            v_sum[pl.ds(first, tall), :] = jnp.where(first_head, v_parts[0], v_parts[1])

        steps = length // tall
        if steps <= UNROLLED:
            for step in range(steps):
                key_step(step * tall, step * tall)
        else:

            @pl.loop(0, steps)
            def _(step):
                key_step(pl.multiple_of(step * tall, tall), 0)

    def give(source, turned, scale):
        for block in range(blocks):
            here = relative_place(block, info_ref, blocks, rows)
            grads = source[pl.ds(block * rows, rows), :] * scale
            if turned:
                grads = grads * cos_ref[here, :] - swap_halves(grads) * sin_ref[here, :]
            back_ref[here, :] = grads.astype(BF16)

    pl.when(kind == 0)(lambda: give(q_sum, True, score_scale))
    pl.when(kind == 1)(lambda: give(k_sum, True, 1.0))
    pl.when(kind == 2)(lambda: give(v_sum, False, 1.0))


def attend_back(info, q_row, k_row, v_row, logs, attended, grads, cosine, sine, blocks):
    length, width = q_row.shape
    pairs = width // PAIR
    one = pl.BlockSpec((length, PAIR), lambda p, c, _: (0, p))
    table = pl.BlockSpec((length, PAIR), lambda p, c, _: (0, 0))
    return pl.pallas_call(
        functools.partial(attend_back_kernel, blocks),
        grid_spec=pltpu.PrefetchScalarGridSpec(
            num_scalar_prefetch=1,
            grid=(pairs, 3),
            in_specs=[one] * 6 + [table] * 2,
            out_specs=pl.BlockSpec((length, PAIR), lambda p, c, _: (0, c * pairs + p)),
            scratch_shapes=[
                pltpu.VMEM((length, PAIR), BF16),
                pltpu.VMEM((length, PAIR), F32),
                pltpu.VMEM((length, PAIR), F32),
                pltpu.VMEM((length, PAIR), F32),
                pltpu.VMEM((8, length), F32),
                pltpu.VMEM((8, length), F32),
            ],
        ),
        out_shape=jax.ShapeDtypeStruct((length, 3 * width), BF16),
        compiler_params=pltpu.CompilerParams(vmem_limit_bytes=48 * 2**20),
        cost_estimate=pl.CostEstimate(
            flops=20 * pairs * length * length * PAIR // 2,
            bytes_accessed=20 * length * width,
            transcendentals=pairs * length * length,
        ),
        name="attend_back",
    )(info, q_row, k_row, v_row, logs, attended, grads, cosine, sine)


def whole_pairs(values, kinds):
    own = values.shape[1] // kinds
    if own % PAIR == 0:
        return values
    values = jnp.pad(values.reshape(-1, kinds, own), ((0, 0), (0, 0), (0, PAIR - own % PAIR)))
    return values.reshape(values.shape[0], -1)


def own_heads(values, kinds, own):
    return values.reshape(values.shape[0], kinds, -1)[:, :, :own].reshape(values.shape[0], -1)


def rms_unit(values):
    factor = lax.rsqrt(jnp.mean(values * values, axis=-1, keepdims=True) + EPSILON)
    return (values * factor, factor)


def norm_back(grad_normed, unit_rows, factor, gain_row):
    scaled_grad = grad_normed * gain_row
    inner_mean = jnp.mean(scaled_grad * unit_rows, axis=-1, keepdims=True)
    return (
        factor * (scaled_grad - unit_rows * inner_mean),
        jnp.sum(grad_normed * unit_rows, axis=0),
    )


def row_layout(lengths, places):
    ends = [jnp.sum(lengths[: i + 1]) for i in range(lengths.shape[0])]
    begins = jnp.zeros_like(places)
    for end in ends:
        begins = jnp.where(places >= end, end, begins)
    return ends, places - begins


def rope_tables(within):
    half = HEAD_DIM // 2
    steps_up = jnp.arange(half, dtype=F32)
    frequency = ROPE_BASE ** (-2.0 * steps_up / HEAD_DIM)
    angles = within.astype(F32)[:, None] * frequency[None, :]
    cosine, sine = jnp.cos(angles), jnp.sin(angles)
    return (
        jnp.concatenate([cosine] * 4, axis=1),
        jnp.concatenate([-sine, sine, -sine, sine], axis=1),
    )


def body(
    tokens, doc_lengths, weight_qkv, weight_out, weight_gate_up, weight_down, norm_gains, cotangent
):
    sizes = [(axis, lax.axis_size(axis)) for axis in ("dp", "blk", "tensor")]
    size_dp, size_blk, size_tensor = (size for _, size in sizes)
    group = size_blk * size_tensor
    local_rows = tokens.shape[1]
    lengths = doc_lengths[0]

    me = (lax.axis_index("blk") * size_tensor + lax.axis_index("tensor")).astype(jnp.int32)
    order = jnp.array([*range(0, group, 2), *range(1, group, 2)], jnp.int32)
    places = (lax.bitwise_xor(order, me)[:, None] * local_rows) + jnp.arange(
        local_rows, dtype=jnp.int32
    )[None, :]
    ends, within = row_layout(lengths, places.reshape(-1))
    info = jnp.stack([me] + ends).astype(jnp.int32)
    cosine, sine = rope_tables(within)

    held_qkv, held_out = named(
        "attention_weights", swap_columns, [weight_qkv, weight_out[:, None, :]], size_blk
    )
    full_qkv = named("qkv_gather", gather_rows, held_qkv)
    gain_pair = named("gain_gather", gather_small, norm_gains, sizes)
    gain_first, gain_second = gain_pair[0], gain_pair[1]

    inputs = tokens[0].astype(F32)
    unit_first, factor_first = rms_unit(inputs)
    normed_first = named("first_spread", spread, (unit_first * gain_first).astype(BF16), PLANE, group)
    held_gate_up, held_down = named(
        "feed_weights", swap_columns, [weight_gate_up, weight_down[:, None, :]], size_blk
    )
    full_out = named("out_gather", gather_rows, held_out, full_qkv, normed_first)
    full_gate_up = named("gate_up_gather", gather_rows, held_gate_up, full_out)
    projected = dot_nn(normed_first, full_qkv)
    features = full_out.shape[1]
    attended, q_row, k_row, v_row, logs = attend(
        info, whole_pairs(projected, 3), cosine, sine, group
    )
    attended_here = own_heads(attended, 1, features)
    branch, _ = named(
        "branch_collect", collect, attended_here, full_out, dot_nt, PLANE, group
    )
    middle = inputs + branch
    unit_second, factor_second = rms_unit(middle)
    normed_second = named("second_spread", spread, (unit_second * gain_second).astype(BF16), PLANE, group)
    hidden_here = full_gate_up.shape[1] // 2
    grad_output = cotangent[0].astype(F32)
    last_rows = cotangent[0]
    if normed_second.shape[0] > LONG_ROW:
        last_rows = after(last_rows, normed_second)
    grad_feed = named("cotangent_spread", spread, last_rows, PLANE, group)
    full_down = named(
        "down_gather", gather_rows, held_down, full_gate_up, normed_second, grad_feed
    )
    gate = dot_nn(normed_second, full_gate_up[:, :hidden_here])
    up = dot_nn(normed_second, full_gate_up[:, hidden_here:])
    sigmoid_gate = jax.nn.sigmoid(gate)
    activated = gate * sigmoid_gate
    hidden = (activated * up).astype(BF16)
    grad_down = dot_tn(grad_feed, hidden).astype(BF16)
    wide = full_down.shape[1]
    full_down = after(full_down, grad_down)
    down_sum = named("down_back", sum_rows, after(grad_down, full_down))
    grad_hidden = dot_nn(grad_feed, full_down)
    silu_slope = sigmoid_gate * (1.0 + gate * (1.0 - sigmoid_gate))
    grad_gates = jnp.concatenate(
        [
            (grad_hidden * up * silu_slope).astype(BF16),
            (grad_hidden * activated).astype(BF16),
        ],
        axis=1,
    )
    grad_gate_up = dot_tn(normed_second, grad_gates).astype(BF16)
    grad_normed_second, first_second = named(
        "second_grad_collect", collect, grad_gates, full_gate_up, dot_nt, PLANE, group
    )
    grad_gate_up = after(grad_gate_up, down_sum, first_second)
    gate_up_sum = named("gate_up_back", sum_rows, grad_gate_up)
    grad_middle_norm, sum_second = norm_back(
        grad_normed_second, unit_second, factor_second, gain_second
    )
    grad_middle = grad_output + grad_middle_norm
    grad_branch = named("branch_grad_spread", spread, grad_middle.astype(BF16), PLANE, group)
    with jax.named_scope("feed_collect"):
        feed_hidden = after(hidden, first_second)
        feed_out, _ = collect(
            feed_hidden, full_down, dot_nt, PLANE, group, begin=(grad_branch,)
        )
    [total_down] = named(
        "down_return", return_columns, after(down_sum, grad_branch), size_blk, [1], wide
    )
    grad_out = dot_tn(grad_branch, attended_here).astype(BF16)
    grad_attended = dot_nn(grad_branch, full_out).astype(BF16)
    grad_projected = attend_back(
        info,
        q_row,
        k_row,
        v_row,
        logs,
        attended,
        whole_pairs(grad_attended, 1),
        cosine,
        sine,
        group,
    )
    grad_projected = own_heads(grad_projected, 3, features)
    grad_qkv = dot_tn(normed_first, grad_projected).astype(BF16)
    grad_normed_first, _, feed_out, total_down = named(
        "first_grad_collect",
        collect,
        grad_projected,
        full_qkv,
        dot_nt,
        PLANE,
        group,
        feed_out,
        total_down,
    )
    both = jnp.concatenate([grad_qkv, grad_out], axis=1)
    both_sum = named("attention_back", sum_rows, after(both, gate_up_sum, grad_normed_first))

    outcome = (middle + feed_out).astype(BF16)
    grad_input_norm, sum_first = norm_back(grad_normed_first, unit_first, factor_first, gain_first)
    grad_input = grad_middle + grad_input_norm
    gain_sums = named("gain_scatter", scatter_small, jnp.stack([sum_first, sum_second]), sizes)
    [total_gate_up] = named(
        "gate_up_return", return_columns, gate_up_sum, size_blk, [2], wide
    )
    both_sum = after(both_sum, total_gate_up, outcome, grad_input, gain_sums)
    total_qkv, total_out = named(
        "attention_return", return_columns, both_sum, size_blk, [3, 1], features
    )
    return (
        outcome[None],
        grad_input[None],
        total_qkv,
        total_out[:, 0],
        total_gate_up,
        total_down[:, 0],
        gain_sums,
    )


def solution(mesh):
    return jax.shard_map(
        body,
        mesh=mesh,
        in_specs=(
            P("dp", ("blk", "tensor"), None),
            P("dp", None),
            P(("dp", "blk"), None, "tensor"),
            P(("dp", "blk"), "tensor"),
            P(("dp", "blk"), None, "tensor"),
            P(("dp", "blk"), "tensor"),
            P(None, ("dp", "blk", "tensor")),
            P("dp", ("blk", "tensor"), None),
        ),
        out_specs=(
            P("dp", ("blk", "tensor"), None),
            P("dp", ("blk", "tensor"), None),
            P(("dp", "blk"), None, "tensor"),
            P(("dp", "blk"), "tensor"),
            P(("dp", "blk"), None, "tensor"),
            P(("dp", "blk"), "tensor"),
            P(None, ("dp", "blk", "tensor")),
        ),
        check_vma=False,
    )
```

```python
import functools

import jax
import jax.numpy as jnp
from jax import lax
from jax.experimental import pallas as pl
from jax.experimental.pallas import tpu as pltpu
from jax.sharding import PartitionSpec as P

HEAD_DIM = 64
PAIR = 2 * HEAD_DIM
EPSILON = 1e-05
ROPE_BASE = 130000.0
NEGATIVE = -1e30
QUERY_BLOCK = 256
UNROLLED = 4
LONG_ROW = 2048
PLANE = ("blk", "tensor")
F32 = jnp.float32
BF16 = jnp.bfloat16


def dot_nn(a, b):
    return lax.dot_general(a, b, (((1,), (0,)), ((), ())), preferred_element_type=F32)


def dot_nt(a, b):
    return lax.dot_general(a, b, (((1,), (1,)), ((), ())), preferred_element_type=F32)


def dot_tn(a, b):
    return lax.dot_general(a, b, (((0,), (0,)), ((), ())), preferred_element_type=F32)


def named(name, function, *args):
    with jax.named_scope(name):
        return function(*args)


def after(value, *events):
    return lax.optimization_barrier((value, *events))[0]


def together(*values):
    return lax.optimization_barrier(values)


def swap_by(value, axes, size, bits):
    return lax.ppermute(value, axes, [(i, i ^ bits) for i in range(size)])


def join_kernel(steps, near_ref, far_ref, out_ref):
    step = pl.program_id(0)

    @pl.when(step < steps)
    def _():
        out_ref[...] = near_ref[...]

    @pl.when(step >= steps)
    def _():
        out_ref[...] = far_ref[...]


def join_halves(near, far):
    rows, width = near.shape
    steps = max(1, rows // 128)
    block = (rows // steps, width)
    return pl.pallas_call(
        functools.partial(join_kernel, steps),
        grid=(2 * steps,),
        in_specs=[
            pl.BlockSpec(block, lambda i: (jnp.minimum(i, steps - 1), 0)),
            pl.BlockSpec(block, lambda i: (jnp.maximum(i - steps, 0), 0)),
        ],
        out_specs=pl.BlockSpec(block, lambda i: (i, 0)),
        out_shape=jax.ShapeDtypeStruct((2 * rows, width), near.dtype),
        cost_estimate=pl.CostEstimate(
            flops=0, bytes_accessed=8 * rows * width, transcendentals=0
        ),
        name="join_halves",
    )(near, far)


def spread(rows, axes, size):
    pieces = [swap_by(rows, axes, size, bits) for bits in range(2, size, 2)]
    near = jnp.concatenate([rows] + pieces, axis=0)
    return join_halves(near, swap_by(near, axes, size, 1)), pieces[-1]


def collect(left, right, product, axes, size, *tied, begin=()):
    half = left.shape[0] // 2
    received = swap_by(product(left[half:], right).astype(BF16), axes, size, 1)
    near = (product(left[:half], right) + received.astype(F32)).astype(BF16)
    if tied:
        near, *tied = together(near, *tied)
    if begin:
        near = after(near, *begin)
    rows = near.shape[0] // (size // 2)
    blocks = [
        swap_by(near[place * rows : (place + 1) * rows], axes, size, 2 * place)
        for place in range(1, size // 2)
    ]
    summed = sum([block.astype(F32) for block in blocks], near[:rows].astype(F32))
    return summed, blocks[-1], *tied


def gather_small(value, axis_sizes):
    for axis, size in reversed(axis_sizes):
        index = lax.axis_index(axis)
        bit = 1
        while bit < size:
            other = swap_by(value, axis, size, bit)
            low = (index & bit) == 0
            value = jnp.concatenate(
                [jnp.where(low, value, other), jnp.where(low, other, value)], axis=1
            )
            bit *= 2
    return value


def scatter_small(value, axis_sizes):
    sizes = [size for _, size in axis_sizes]
    kinds = value.shape[0]
    value = value.reshape(kinds, sizes[0], -1).swapaxes(1, 2).reshape(kinds, *sizes[1:], -1)
    value = value.reshape(kinds, -1, value.shape[-1] // sizes[0], sizes[0])
    value = value.swapaxes(2, 3).reshape(kinds, -1)
    for axis, size in (*axis_sizes[1:], axis_sizes[0]):
        index = lax.axis_index(axis)
        bit = size // 2
        while bit >= 1:
            half = value.shape[1] // 2
            low = (index & bit) == 0
            kept = jnp.where(low, value[:, :half], value[:, half:])
            sent = jnp.where(low, value[:, half:], value[:, :half])
            value = kept + swap_by(sent, axis, size, bit)
            bit //= 2
    return value


def trade(blocks, axis):
    return lax.all_to_all(blocks, axis, 0, 0, tiled=True)


def split_columns(weight, blocks):
    rows, kinds, columns = weight.shape
    parted = weight.reshape(rows, kinds, blocks, columns // blocks).transpose(2, 0, 1, 3)
    return parted.reshape(blocks, rows, -1)


def swap_columns(weights, blocks):
    parts = [split_columns(weight, blocks) for weight in weights]
    traded = trade(jnp.concatenate(parts, axis=2), "blk")
    traded = traded.reshape(-1, traded.shape[2])
    cuts = []
    start = 0
    for part in parts:
        cuts.append(traded[:, start : start + part.shape[2]])
        start += part.shape[2]
    return cuts


def gather_rows(weight, *events):
    return lax.all_gather(after(weight, *events), "dp", axis=0, tiled=True)


def sum_rows(grads):
    return lax.psum_scatter(grads, "dp", scatter_dimension=0, tiled=True)


def return_columns(summed, blocks, kinds, own):
    parted = trade(summed.reshape(blocks, -1, summed.shape[1]), "blk").astype(F32)
    totals = []
    start = 0
    for kind in kinds:
        columns = [
            [parted[b, :, start + i * own : start + (i + 1) * own] for b in range(blocks)]
            for i in range(kind)
        ]
        totals.append(jnp.stack([jnp.concatenate(part, axis=1) for part in columns], axis=1))
        start += kind * own
    return totals


def swap_halves(values):
    lane = lax.broadcasted_iota(jnp.int32, values.shape, 1)
    half = HEAD_DIM // 2
    return jnp.where(
        lane % HEAD_DIM < half,
        pltpu.roll(values, PAIR - half, 1),
        pltpu.roll(values, half, 1),
    )


def relative_place(block, info_ref, blocks, rows):
    bits = lax.bitwise_xor(jnp.int32(block), info_ref[0])
    place = lax.shift_right_logical(bits, 1) + (bits & 1) * (blocks // 2)
    return pl.ds(pl.multiple_of(place * rows, rows), rows)


def document_start(places, info_ref):
    end_0 = info_ref[1]
    end_1 = info_ref[2]
    end_2 = info_ref[3]
    start = jnp.where(places >= end_0, end_0, 0)
    start = jnp.where(places >= end_1, end_1, start)
    return jnp.where(places >= end_2, end_2, start)


def head_lanes(shape, head):
    lane = lax.broadcasted_iota(jnp.int32, shape, 1)
    return (lane < HEAD_DIM) if head == 0 else (lane >= HEAD_DIM)


def only_head(values, head):
    return jnp.where(head_lanes(values.shape, head), values, jnp.zeros_like(values))


def attend_kernel(
    blocks,
    info_ref,
    q_ref,
    k_ref,
    v_ref,
    cos_ref,
    sin_ref,
    out_ref,
    q_row,
    k_row,
    v_row,
    log_ref,
):
    length = q_ref.shape[0]
    rows = length // blocks
    score_scale = HEAD_DIM ** (-0.5)
    for block in range(blocks):
        here = relative_place(block, info_ref, blocks, rows)
        there = pl.ds(block * rows, rows)
        cosine, sine = cos_ref[here, :], sin_ref[here, :]
        q, k = q_ref[here, :], k_ref[here, :]
        q_row[there, :] = ((q * cosine + swap_halves(q) * sine) * score_scale).astype(BF16)
        k_row[there, :] = (k * cosine + swap_halves(k) * sine).astype(BF16)
        v_row[there, :] = v_ref[here, :].astype(BF16)

    tall = max(QUERY_BLOCK, rows)

    def query_step(first, width):
        queries = q_row[pl.ds(first, tall), :]
        places = first + lax.broadcasted_iota(jnp.int32, (tall, 1), 0)
        keys_at = lax.broadcasted_iota(jnp.int32, (tall, width), 1)
        allowed = (keys_at <= places) & (keys_at >= document_start(places, info_ref))
        results = []
        logs = []
        for head in range(2):
            scores = dot_nt(only_head(queries, head), k_row[:width, :])
            scores = jnp.where(allowed, scores, NEGATIVE)
            highest = jnp.max(scores, axis=1, keepdims=True)
            weights = jnp.exp(scores - highest)
            total = jnp.sum(weights, axis=1, keepdims=True)
            results.append(dot_nn(weights.astype(BF16), v_row[:width, :]) / total)
            logs.append(highest + jnp.log(total))
        first_head = head_lanes((tall, PAIR), 0)
        present = (places < info_ref[3]).astype(F32)
        merged = (jnp.where(first_head, results[0], results[1]) * present).astype(BF16)
        log_ref[pl.ds(first, tall), :] = jnp.where(first_head, logs[0], logs[1])
        return merged

    def put(merged, first_block):
        for part in range(tall // rows):
            here = relative_place(first_block + part, info_ref, blocks, rows)
            out_ref[here, :] = merged[part * rows : (part + 1) * rows]

    steps = length // tall
    if steps <= UNROLLED:
        for step in range(steps):
            put(query_step(step * tall, (step + 1) * tall), step * (tall // rows))
    else:

        @pl.loop(0, steps)
        def _(step):
            put(query_step(pl.multiple_of(step * tall, tall), length), step * (tall // rows))


def attend(info, projected, cosine, sine, blocks):
    length, width = projected.shape
    pairs = width // 3 // PAIR
    whole = lambda kind: pl.BlockSpec((length, PAIR), lambda p, _: (0, kind * pairs + p))
    table = pl.BlockSpec((length, PAIR), lambda p, _: (0, 0))
    shape = lambda kind: jax.ShapeDtypeStruct((length, pairs * PAIR), kind)
    return pl.pallas_call(
        functools.partial(attend_kernel, blocks),
        grid_spec=pltpu.PrefetchScalarGridSpec(
            num_scalar_prefetch=1,
            grid=(pairs,),
            in_specs=[whole(0), whole(1), whole(2), table, table],
            out_specs=[whole(0)] * 5,
        ),
        out_shape=[shape(BF16), shape(BF16), shape(BF16), shape(BF16), shape(F32)],
        compiler_params=pltpu.CompilerParams(vmem_limit_bytes=48 * 2**20),
        cost_estimate=pl.CostEstimate(
            flops=8 * pairs * length * length * PAIR // 2,
            bytes_accessed=6 * length * width,
            transcendentals=pairs * length * length,
        ),
        name="attend",
    )(info, projected, projected, projected, cosine, sine)


def attend_back_kernel(
    blocks,
    info_ref,
    q_row,
    k_row,
    v_row,
    log_ref,
    out_ref,
    grad_ref,
    cos_ref,
    sin_ref,
    back_ref,
    g_row,
    q_sum,
    k_sum,
    v_sum,
    log_flat,
    inner_flat,
):
    length = q_row.shape[0]
    rows = length // blocks
    score_scale = HEAD_DIM ** (-0.5)
    kind = pl.program_id(1)
    tall = max(QUERY_BLOCK, rows)

    @pl.when(kind == 0)
    def _():
        for block in range(blocks):
            here = relative_place(block, info_ref, blocks, rows)
            there = pl.ds(block * rows, rows)
            places = block * rows + lax.broadcasted_iota(jnp.int32, (rows, 1), 0)
            present = (places < info_ref[3]).astype(F32)
            grads = grad_ref[here, :].astype(F32) * present
            g_row[there, :] = grads.astype(BF16)
            inner = (grads * out_ref[here, :].astype(F32)).T
            for head in range(2):
                span = slice(head * HEAD_DIM, (head + 1) * HEAD_DIM)
                inner_flat[head : head + 1, there] = jnp.sum(inner[span], axis=0, keepdims=True)
            logs = log_ref[there, :].T
            for head in range(2):
                log_flat[head : head + 1, there] = logs[head * HEAD_DIM : head * HEAD_DIM + 1]
        q_sum[...] = jnp.zeros_like(q_sum)

        def key_step(first, from_query):
            width = length - from_query
            span = slice(from_query, length)
            keys = k_row[pl.ds(first, tall), :]
            values = v_row[pl.ds(first, tall), :]
            keys_at = first + lax.broadcasted_iota(jnp.int32, (tall, 1), 0)
            places = from_query + lax.broadcasted_iota(jnp.int32, (1, width), 1)
            allowed = (keys_at <= places) & (keys_at >= document_start(places, info_ref))
            queries, grads = q_row[span, :], g_row[span, :]
            k_parts = []
            v_parts = []
            for head in range(2):
                keys_head = only_head(keys, head)
                scores = dot_nt(keys_head, queries)
                raised = jnp.exp(scores - log_flat[head : head + 1, span])
                weights = jnp.where(allowed, raised, 0.0)
                grad_weights = dot_nt(only_head(values, head), grads)
                grad_scores = weights * (grad_weights - inner_flat[head : head + 1, span])
                grad_scores = grad_scores.astype(BF16)
                v_parts.append(dot_nn(weights.astype(BF16), grads))
                k_parts.append(dot_nn(grad_scores, queries))
                q_sum[span, :] += dot_tn(grad_scores, keys_head)
            first_head = head_lanes((tall, PAIR), 0)
            k_sum[pl.ds(first, tall), :] = jnp.where(first_head, k_parts[0], k_parts[1])
            v_sum[pl.ds(first, tall), :] = jnp.where(first_head, v_parts[0], v_parts[1])

        steps = length // tall
        if steps <= UNROLLED:
            for step in range(steps):
                key_step(step * tall, step * tall)
        else:

            @pl.loop(0, steps)
            def _(step):
                key_step(pl.multiple_of(step * tall, tall), 0)

    def give(source, turned, scale):
        for block in range(blocks):
            here = relative_place(block, info_ref, blocks, rows)
            grads = source[pl.ds(block * rows, rows), :] * scale
            if turned:
                grads = grads * cos_ref[here, :] - swap_halves(grads) * sin_ref[here, :]
            back_ref[here, :] = grads.astype(BF16)

    pl.when(kind == 0)(lambda: give(q_sum, True, score_scale))
    pl.when(kind == 1)(lambda: give(k_sum, True, 1.0))
    pl.when(kind == 2)(lambda: give(v_sum, False, 1.0))


def attend_back(info, q_row, k_row, v_row, logs, attended, grads, cosine, sine, blocks):
    length, width = q_row.shape
    pairs = width // PAIR
    one = pl.BlockSpec((length, PAIR), lambda p, c, _: (0, p))
    table = pl.BlockSpec((length, PAIR), lambda p, c, _: (0, 0))
    return pl.pallas_call(
        functools.partial(attend_back_kernel, blocks),
        grid_spec=pltpu.PrefetchScalarGridSpec(
            num_scalar_prefetch=1,
            grid=(pairs, 3),
            in_specs=[one] * 6 + [table] * 2,
            out_specs=pl.BlockSpec((length, PAIR), lambda p, c, _: (0, c * pairs + p)),
            scratch_shapes=[
                pltpu.VMEM((length, PAIR), BF16),
                pltpu.VMEM((length, PAIR), F32),
                pltpu.VMEM((length, PAIR), F32),
                pltpu.VMEM((length, PAIR), F32),
                pltpu.VMEM((8, length), F32),
                pltpu.VMEM((8, length), F32),
            ],
        ),
        out_shape=jax.ShapeDtypeStruct((length, 3 * width), BF16),
        compiler_params=pltpu.CompilerParams(vmem_limit_bytes=48 * 2**20),
        cost_estimate=pl.CostEstimate(
            flops=20 * pairs * length * length * PAIR // 2,
            bytes_accessed=20 * length * width,
            transcendentals=pairs * length * length,
        ),
        name="attend_back",
    )(info, q_row, k_row, v_row, logs, attended, grads, cosine, sine)


def whole_pairs(values, kinds):
    own = values.shape[1] // kinds
    if own % PAIR == 0:
        return values
    values = jnp.pad(values.reshape(-1, kinds, own), ((0, 0), (0, 0), (0, PAIR - own % PAIR)))
    return values.reshape(values.shape[0], -1)


def own_heads(values, kinds, own):
    return values.reshape(values.shape[0], kinds, -1)[:, :, :own].reshape(values.shape[0], -1)


def rms_unit(values):
    factor = lax.rsqrt(jnp.mean(values * values, axis=-1, keepdims=True) + EPSILON)
    return (values * factor, factor)


def norm_back(grad_normed, unit_rows, factor, gain_row):
    scaled_grad = grad_normed * gain_row
    inner_mean = jnp.mean(scaled_grad * unit_rows, axis=-1, keepdims=True)
    return (
        factor * (scaled_grad - unit_rows * inner_mean),
        jnp.sum(grad_normed * unit_rows, axis=0),
    )


def row_layout(lengths, places):
    ends = [jnp.sum(lengths[: i + 1]) for i in range(lengths.shape[0])]
    begins = jnp.zeros_like(places)
    for end in ends:
        begins = jnp.where(places >= end, end, begins)
    return ends, places - begins


def rope_tables(within):
    half = HEAD_DIM // 2
    steps_up = jnp.arange(half, dtype=F32)
    frequency = ROPE_BASE ** (-2.0 * steps_up / HEAD_DIM)
    angles = within.astype(F32)[:, None] * frequency[None, :]
    cosine, sine = jnp.cos(angles), jnp.sin(angles)
    return (
        jnp.concatenate([cosine] * 4, axis=1),
        jnp.concatenate([-sine, sine, -sine, sine], axis=1),
    )


def body(
    tokens, doc_lengths, weight_qkv, weight_out, weight_gate_up, weight_down, norm_gains, cotangent
):
    sizes = [(axis, lax.axis_size(axis)) for axis in ("dp", "blk", "tensor")]
    size_dp, size_blk, size_tensor = (size for _, size in sizes)
    group = size_blk * size_tensor
    local_rows = tokens.shape[1]
    lengths = doc_lengths[0]

    me = (lax.axis_index("blk") * size_tensor + lax.axis_index("tensor")).astype(jnp.int32)
    order = jnp.array([*range(0, group, 2), *range(1, group, 2)], jnp.int32)
    places = (lax.bitwise_xor(order, me)[:, None] * local_rows) + jnp.arange(
        local_rows, dtype=jnp.int32
    )[None, :]
    ends, within = row_layout(lengths, places.reshape(-1))
    info = jnp.stack([me] + ends).astype(jnp.int32)
    cosine, sine = rope_tables(within)

    held_attention = named(
        "attention_weights", swap_columns, [weight_qkv, weight_out[:, None, :]], size_blk
    )
    full_attention = jnp.concatenate(held_attention, axis=1)
    full_attention = named("attention_gather", gather_rows, full_attention)
    cut = held_attention[0].shape[1]
    full_qkv, full_out = full_attention[:, :cut], full_attention[:, cut:]
    held_gate_up, held_down = named(
        "feed_weights",
        swap_columns,
        [after(weight_gate_up, *held_attention), weight_down[:, None, :]],
        size_blk,
    )
    gain_pair = named("gain_gather", gather_small, norm_gains, sizes)
    gain_first, gain_second = gain_pair[0], gain_pair[1]

    inputs = tokens[0].astype(F32)
    unit_first, factor_first = rms_unit(inputs)
    rows_first = (unit_first * gain_first).astype(BF16)
    rows_first, held_gate_up, held_down = together(rows_first, held_gate_up, held_down)
    normed_first, last_first = named("first_spread", spread, rows_first, PLANE, group)
    full_gate_up = named(
        "gate_up_gather", gather_rows, held_gate_up, full_attention, last_first
    )
    projected = dot_nn(normed_first, full_qkv)
    features = full_out.shape[1]
    attended, q_row, k_row, v_row, logs = attend(
        info, whole_pairs(projected, 3), cosine, sine, group
    )
    attended_here = own_heads(attended, 1, features)
    branch, _ = named(
        "branch_collect", collect, attended_here, full_out, dot_nt, PLANE, group
    )
    middle = inputs + branch
    unit_second, factor_second = rms_unit(middle)
    normed_second, _ = named("second_spread", spread, (unit_second * gain_second).astype(BF16), PLANE, group)
    hidden_here = full_gate_up.shape[1] // 2
    grad_output = cotangent[0].astype(F32)
    last_rows = cotangent[0]
    if normed_second.shape[0] > LONG_ROW:
        last_rows = after(last_rows, normed_second)
    grad_feed, _ = named("cotangent_spread", spread, last_rows, PLANE, group)
    full_down = named(
        "down_gather", gather_rows, held_down, full_gate_up, normed_second, grad_feed
    )
    gate = dot_nn(normed_second, full_gate_up[:, :hidden_here])
    up = dot_nn(normed_second, full_gate_up[:, hidden_here:])
    sigmoid_gate = jax.nn.sigmoid(gate)
    activated = gate * sigmoid_gate
    hidden = (activated * up).astype(BF16)
    grad_down = dot_tn(grad_feed, hidden).astype(BF16)
    wide = full_down.shape[1]
    full_down = after(full_down, grad_down)
    down_sum = named("down_back", sum_rows, after(grad_down, full_down))
    grad_hidden = dot_nn(grad_feed, full_down)
    silu_slope = sigmoid_gate * (1.0 + gate * (1.0 - sigmoid_gate))
    grad_gates = jnp.concatenate(
        [
            (grad_hidden * up * silu_slope).astype(BF16),
            (grad_hidden * activated).astype(BF16),
        ],
        axis=1,
    )
    grad_gate_up = dot_tn(normed_second, grad_gates).astype(BF16)
    grad_normed_second, last_second = named(
        "second_grad_collect", collect, grad_gates, full_gate_up, dot_nt, PLANE, group
    )
    grad_gate_up = after(grad_gate_up, down_sum, last_second)
    gate_up_sum = named("gate_up_back", sum_rows, grad_gate_up)
    grad_middle_norm, sum_second = norm_back(
        grad_normed_second, unit_second, factor_second, gain_second
    )
    grad_middle = grad_output + grad_middle_norm
    grad_branch, _ = named("branch_grad_spread", spread, grad_middle.astype(BF16), PLANE, group)
    with jax.named_scope("feed_collect"):
        feed_hidden = after(hidden, last_second)
        feed_out, _ = collect(
            feed_hidden, full_down, dot_nt, PLANE, group, begin=(grad_branch,)
        )
    [total_down] = named(
        "down_return", return_columns, after(down_sum, grad_branch), size_blk, [1], wide
    )
    grad_out = dot_tn(grad_branch, attended_here).astype(BF16)
    grad_attended = dot_nn(grad_branch, full_out).astype(BF16)
    grad_projected = attend_back(
        info,
        q_row,
        k_row,
        v_row,
        logs,
        attended,
        whole_pairs(grad_attended, 1),
        cosine,
        sine,
        group,
    )
    grad_projected = own_heads(grad_projected, 3, features)
    grad_qkv = dot_tn(normed_first, grad_projected).astype(BF16)
    grad_normed_first, last_grad = named(
        "first_grad_collect", collect, grad_projected, full_qkv, dot_nt, PLANE, group
    )
    both = jnp.concatenate([grad_qkv, grad_out], axis=1)
    both_sum = named("attention_back", sum_rows, after(both, gate_up_sum, last_grad))

    outcome = (middle + feed_out).astype(BF16)
    grad_input_norm, sum_first = norm_back(grad_normed_first, unit_first, factor_first, gain_first)
    grad_input = grad_middle + grad_input_norm
    gain_sums = named("gain_scatter", scatter_small, jnp.stack([sum_first, sum_second]), sizes)
    [total_gate_up] = named(
        "gate_up_return", return_columns, gate_up_sum, size_blk, [2], wide
    )
    both_sum = after(both_sum, total_gate_up, total_down, outcome, grad_input, gain_sums)
    total_qkv, total_out = named(
        "attention_return", return_columns, both_sum, size_blk, [3, 1], features
    )
    return (
        outcome[None],
        grad_input[None],
        total_qkv,
        total_out[:, 0],
        total_gate_up,
        total_down[:, 0],
        gain_sums,
    )


def solution(mesh):
    return jax.shard_map(
        body,
        mesh=mesh,
        in_specs=(
            P("dp", ("blk", "tensor"), None),
            P("dp", None),
            P(("dp", "blk"), None, "tensor"),
            P(("dp", "blk"), "tensor"),
            P(("dp", "blk"), None, "tensor"),
            P(("dp", "blk"), "tensor"),
            P(None, ("dp", "blk", "tensor")),
            P("dp", ("blk", "tensor"), None),
        ),
        out_specs=(
            P("dp", ("blk", "tensor"), None),
            P("dp", ("blk", "tensor"), None),
            P(("dp", "blk"), None, "tensor"),
            P(("dp", "blk"), "tensor"),
            P(("dp", "blk"), None, "tensor"),
            P(("dp", "blk"), "tensor"),
            P(None, ("dp", "blk", "tensor")),
        ),
        check_vma=False,
    )
```

```python
import functools

import jax
import jax.numpy as jnp
from jax import lax
from jax.experimental import pallas as pl
from jax.experimental.pallas import tpu as pltpu
from jax.sharding import PartitionSpec as P

HEAD_DIM = 64
PAIR = 2 * HEAD_DIM
EPSILON = 1e-05
ROPE_BASE = 130000.0
NEGATIVE = -1e30
QUERY_BLOCK = 256
UNROLLED = 4
LONG_ROW = 2048
PLANE = ("blk", "tensor")
F32 = jnp.float32
BF16 = jnp.bfloat16


def dot_nn(a, b):
    return lax.dot_general(a, b, (((1,), (0,)), ((), ())), preferred_element_type=F32)


def dot_nt(a, b):
    return lax.dot_general(a, b, (((1,), (1,)), ((), ())), preferred_element_type=F32)


def dot_tn(a, b):
    return lax.dot_general(a, b, (((0,), (0,)), ((), ())), preferred_element_type=F32)


def named(name, function, *args):
    with jax.named_scope(name):
        return function(*args)


def after(value, *events):
    return lax.optimization_barrier((value, *events))[0]


def together(*values):
    return lax.optimization_barrier(values)


def swap_by(value, axes, size, bits):
    return lax.ppermute(value, axes, [(i, i ^ bits) for i in range(size)])


def join_kernel(steps, near_ref, far_ref, out_ref):
    step = pl.program_id(0)

    @pl.when(step < steps)
    def _():
        out_ref[...] = near_ref[...]

    @pl.when(step >= steps)
    def _():
        out_ref[...] = far_ref[...]


def join_halves(near, far):
    rows, width = near.shape
    steps = max(1, rows // 128)
    block = (rows // steps, width)
    return pl.pallas_call(
        functools.partial(join_kernel, steps),
        grid=(2 * steps,),
        in_specs=[
            pl.BlockSpec(block, lambda i: (jnp.minimum(i, steps - 1), 0)),
            pl.BlockSpec(block, lambda i: (jnp.maximum(i - steps, 0), 0)),
        ],
        out_specs=pl.BlockSpec(block, lambda i: (i, 0)),
        out_shape=jax.ShapeDtypeStruct((2 * rows, width), near.dtype),
        cost_estimate=pl.CostEstimate(
            flops=0, bytes_accessed=8 * rows * width, transcendentals=0
        ),
        name="join_halves",
    )(near, far)


def spread(rows, axes, size):
    pieces = [swap_by(rows, axes, size, bits) for bits in range(2, size, 2)]
    near = jnp.concatenate([rows] + pieces, axis=0)
    return join_halves(near, swap_by(near, axes, size, 1)), pieces[-1]


def collect(left, right, product, axes, size, begin=()):
    half = left.shape[0] // 2
    received = swap_by(product(left[half:], right).astype(BF16), axes, size, 1)
    near = (product(left[:half], right) + received.astype(F32)).astype(BF16)
    if begin:
        near = after(near, *begin)
    rows = near.shape[0] // (size // 2)
    blocks = [
        swap_by(near[place * rows : (place + 1) * rows], axes, size, 2 * place)
        for place in range(1, size // 2)
    ]
    summed = sum([block.astype(F32) for block in blocks], near[:rows].astype(F32))
    return summed, blocks


def gather_small(value, axis_sizes):
    for axis, size in reversed(axis_sizes):
        index = lax.axis_index(axis)
        bit = 1
        while bit < size:
            other = swap_by(value, axis, size, bit)
            low = (index & bit) == 0
            value = jnp.concatenate(
                [jnp.where(low, value, other), jnp.where(low, other, value)], axis=1
            )
            bit *= 2
    return value


def scatter_small(value, axis_sizes):
    sizes = [size for _, size in axis_sizes]
    kinds = value.shape[0]
    value = value.reshape(kinds, sizes[0], -1).swapaxes(1, 2).reshape(kinds, *sizes[1:], -1)
    value = value.reshape(kinds, -1, value.shape[-1] // sizes[0], sizes[0])
    value = value.swapaxes(2, 3).reshape(kinds, -1)
    for axis, size in (*axis_sizes[1:], axis_sizes[0]):
        index = lax.axis_index(axis)
        bit = size // 2
        while bit >= 1:
            half = value.shape[1] // 2
            low = (index & bit) == 0
            kept = jnp.where(low, value[:, :half], value[:, half:])
            sent = jnp.where(low, value[:, half:], value[:, :half])
            value = kept + swap_by(sent, axis, size, bit)
            bit //= 2
    return value


def trade(blocks, axis):
    return lax.all_to_all(blocks, axis, 0, 0, tiled=True)


def split_columns(weight, blocks):
    rows, kinds, columns = weight.shape
    parted = weight.reshape(rows, kinds, blocks, columns // blocks).transpose(2, 0, 1, 3)
    return parted.reshape(blocks, rows, -1)


def swap_columns(weights, blocks):
    parts = [split_columns(weight, blocks) for weight in weights]
    traded = trade(jnp.concatenate(parts, axis=2), "blk")
    traded = traded.reshape(-1, traded.shape[2])
    cuts = []
    start = 0
    for part in parts:
        cuts.append(traded[:, start : start + part.shape[2]])
        start += part.shape[2]
    return cuts


def gather_rows(weight, *events):
    return lax.all_gather(after(weight, *events), "dp", axis=0, tiled=True)


def sum_rows(grads):
    return lax.psum_scatter(grads, "dp", scatter_dimension=0, tiled=True)


def return_columns(summed, blocks, kinds, wide):
    parted = summed.reshape(blocks, -1, summed.shape[1])
    if blocks == 2:
        first = lax.axis_index("blk") == 0
        got = swap_by(jnp.where(first, parted[1], parted[0]), "blk", blocks, 1).astype(F32)
        own = jnp.where(first, parted[0], parted[1]).astype(F32)
        parted = [jnp.where(first, own, got), jnp.where(first, got, own)]
    else:
        parted = list(trade(parted, "blk").astype(F32))
    totals = []
    start = 0
    for kind in kinds:
        columns = [
            [parted[b][:, start + i * wide : start + (i + 1) * wide] for b in range(blocks)]
            for i in range(kind)
        ]
        totals.append(jnp.stack([jnp.concatenate(part, axis=1) for part in columns], axis=1))
        start += kind * wide
    return totals


def swap_halves(values):
    lane = lax.broadcasted_iota(jnp.int32, values.shape, 1)
    half = HEAD_DIM // 2
    return jnp.where(
        lane % HEAD_DIM < half,
        pltpu.roll(values, PAIR - half, 1),
        pltpu.roll(values, half, 1),
    )


def relative_place(block, info_ref, blocks, rows):
    bits = lax.bitwise_xor(jnp.int32(block), info_ref[0])
    place = lax.shift_right_logical(bits, 1) + (bits & 1) * (blocks // 2)
    return pl.ds(pl.multiple_of(place * rows, rows), rows)


def document_start(places, info_ref):
    end_0 = info_ref[1]
    end_1 = info_ref[2]
    end_2 = info_ref[3]
    start = jnp.where(places >= end_0, end_0, 0)
    start = jnp.where(places >= end_1, end_1, start)
    return jnp.where(places >= end_2, end_2, start)


def head_lanes(shape, head):
    lane = lax.broadcasted_iota(jnp.int32, shape, 1)
    return (lane < HEAD_DIM) if head == 0 else (lane >= HEAD_DIM)


def only_head(values, head):
    return jnp.where(head_lanes(values.shape, head), values, jnp.zeros_like(values))


def attend_kernel(
    blocks,
    info_ref,
    q_ref,
    k_ref,
    v_ref,
    cos_ref,
    sin_ref,
    out_ref,
    q_row,
    k_row,
    v_row,
    log_ref,
):
    length = q_ref.shape[0]
    rows = length // blocks
    score_scale = HEAD_DIM ** (-0.5)
    for block in range(blocks):
        here = relative_place(block, info_ref, blocks, rows)
        there = pl.ds(block * rows, rows)
        cosine, sine = cos_ref[here, :], sin_ref[here, :]
        q, k = q_ref[here, :], k_ref[here, :]
        q_row[there, :] = ((q * cosine + swap_halves(q) * sine) * score_scale).astype(BF16)
        k_row[there, :] = (k * cosine + swap_halves(k) * sine).astype(BF16)
        v_row[there, :] = v_ref[here, :].astype(BF16)

    tall = max(QUERY_BLOCK, rows)

    def query_step(first, width):
        queries = q_row[pl.ds(first, tall), :]
        places = first + lax.broadcasted_iota(jnp.int32, (tall, 1), 0)
        keys_at = lax.broadcasted_iota(jnp.int32, (tall, width), 1)
        allowed = (keys_at <= places) & (keys_at >= document_start(places, info_ref))
        results = []
        logs = []
        for head in range(2):
            scores = dot_nt(only_head(queries, head), k_row[:width, :])
            scores = jnp.where(allowed, scores, NEGATIVE)
            highest = jnp.max(scores, axis=1, keepdims=True)
            weights = jnp.exp(scores - highest)
            total = jnp.sum(weights, axis=1, keepdims=True)
            results.append(dot_nn(weights.astype(BF16), v_row[:width, :]) / total)
            logs.append(highest + jnp.log(total))
        first_head = head_lanes((tall, PAIR), 0)
        present = (places < info_ref[3]).astype(F32)
        merged = (jnp.where(first_head, results[0], results[1]) * present).astype(BF16)
        log_ref[pl.ds(first, tall), :] = jnp.where(first_head, logs[0], logs[1])
        return merged

    def put(merged, first_block):
        for part in range(tall // rows):
            here = relative_place(first_block + part, info_ref, blocks, rows)
            out_ref[here, :] = merged[part * rows : (part + 1) * rows]

    steps = length // tall
    if steps <= UNROLLED:
        for step in range(steps):
            put(query_step(step * tall, (step + 1) * tall), step * (tall // rows))
    else:

        @pl.loop(0, steps)
        def _(step):
            put(query_step(pl.multiple_of(step * tall, tall), length), step * (tall // rows))


def attend(info, projected, cosine, sine, blocks):
    length, width = projected.shape
    pairs = width // 3 // PAIR
    whole = lambda kind: pl.BlockSpec((length, PAIR), lambda p, _: (0, kind * pairs + p))
    table = pl.BlockSpec((length, PAIR), lambda p, _: (0, 0))
    shape = lambda kind: jax.ShapeDtypeStruct((length, pairs * PAIR), kind)
    return pl.pallas_call(
        functools.partial(attend_kernel, blocks),
        grid_spec=pltpu.PrefetchScalarGridSpec(
            num_scalar_prefetch=1,
            grid=(pairs,),
            in_specs=[whole(0), whole(1), whole(2), table, table],
            out_specs=[whole(0)] * 5,
        ),
        out_shape=[shape(BF16), shape(BF16), shape(BF16), shape(BF16), shape(F32)],
        compiler_params=pltpu.CompilerParams(vmem_limit_bytes=48 * 2**20),
        cost_estimate=pl.CostEstimate(
            flops=8 * pairs * length * length * PAIR // 2,
            bytes_accessed=6 * length * width,
            transcendentals=pairs * length * length,
        ),
        name="attend",
    )(info, projected, projected, projected, cosine, sine)


def attend_back_kernel(
    blocks,
    info_ref,
    q_row,
    k_row,
    v_row,
    log_ref,
    out_ref,
    grad_ref,
    cos_ref,
    sin_ref,
    back_ref,
    g_row,
    q_sum,
    k_sum,
    v_sum,
    log_flat,
    inner_flat,
):
    length = q_row.shape[0]
    rows = length // blocks
    score_scale = HEAD_DIM ** (-0.5)
    kind = pl.program_id(1)
    tall = max(QUERY_BLOCK, rows)

    @pl.when(kind == 0)
    def _():
        for block in range(blocks):
            here = relative_place(block, info_ref, blocks, rows)
            there = pl.ds(block * rows, rows)
            places = block * rows + lax.broadcasted_iota(jnp.int32, (rows, 1), 0)
            present = (places < info_ref[3]).astype(F32)
            grads = grad_ref[here, :].astype(F32) * present
            g_row[there, :] = grads.astype(BF16)
            inner = (grads * out_ref[here, :].astype(F32)).T
            for head in range(2):
                span = slice(head * HEAD_DIM, (head + 1) * HEAD_DIM)
                inner_flat[head : head + 1, there] = jnp.sum(inner[span], axis=0, keepdims=True)
            logs = log_ref[there, :].T
            for head in range(2):
                log_flat[head : head + 1, there] = logs[head * HEAD_DIM : head * HEAD_DIM + 1]
        q_sum[...] = jnp.zeros_like(q_sum)

        def key_step(first, from_query):
            width = length - from_query
            span = slice(from_query, length)
            keys = k_row[pl.ds(first, tall), :]
            values = v_row[pl.ds(first, tall), :]
            keys_at = first + lax.broadcasted_iota(jnp.int32, (tall, 1), 0)
            places = from_query + lax.broadcasted_iota(jnp.int32, (1, width), 1)
            allowed = (keys_at <= places) & (keys_at >= document_start(places, info_ref))
            queries, grads = q_row[span, :], g_row[span, :]
            k_parts = []
            v_parts = []
            for head in range(2):
                keys_head = only_head(keys, head)
                scores = dot_nt(keys_head, queries)
                raised = jnp.exp(scores - log_flat[head : head + 1, span])
                weights = jnp.where(allowed, raised, 0.0)
                grad_weights = dot_nt(only_head(values, head), grads)
                grad_scores = weights * (grad_weights - inner_flat[head : head + 1, span])
                grad_scores = grad_scores.astype(BF16)
                v_parts.append(dot_nn(weights.astype(BF16), grads))
                k_parts.append(dot_nn(grad_scores, queries))
                q_sum[span, :] += dot_tn(grad_scores, keys_head)
            first_head = head_lanes((tall, PAIR), 0)
            k_sum[pl.ds(first, tall), :] = jnp.where(first_head, k_parts[0], k_parts[1])
            v_sum[pl.ds(first, tall), :] = jnp.where(first_head, v_parts[0], v_parts[1])

        steps = length // tall
        if steps <= UNROLLED:
            for step in range(steps):
                key_step(step * tall, step * tall)
        else:

            @pl.loop(0, steps)
            def _(step):
                key_step(pl.multiple_of(step * tall, tall), 0)

    def give(source, turned, scale):
        for block in range(blocks):
            here = relative_place(block, info_ref, blocks, rows)
            grads = source[pl.ds(block * rows, rows), :] * scale
            if turned:
                grads = grads * cos_ref[here, :] - swap_halves(grads) * sin_ref[here, :]
            back_ref[here, :] = grads.astype(BF16)

    pl.when(kind == 0)(lambda: give(q_sum, True, score_scale))
    pl.when(kind == 1)(lambda: give(k_sum, True, 1.0))
    pl.when(kind == 2)(lambda: give(v_sum, False, 1.0))


def attend_back(info, q_row, k_row, v_row, logs, attended, grads, cosine, sine, blocks):
    length, width = q_row.shape
    pairs = width // PAIR
    one = pl.BlockSpec((length, PAIR), lambda p, c, _: (0, p))
    table = pl.BlockSpec((length, PAIR), lambda p, c, _: (0, 0))
    return pl.pallas_call(
        functools.partial(attend_back_kernel, blocks),
        grid_spec=pltpu.PrefetchScalarGridSpec(
            num_scalar_prefetch=1,
            grid=(pairs, 3),
            in_specs=[one] * 6 + [table] * 2,
            out_specs=pl.BlockSpec((length, PAIR), lambda p, c, _: (0, c * pairs + p)),
            scratch_shapes=[
                pltpu.VMEM((length, PAIR), BF16),
                pltpu.VMEM((length, PAIR), F32),
                pltpu.VMEM((length, PAIR), F32),
                pltpu.VMEM((length, PAIR), F32),
                pltpu.VMEM((8, length), F32),
                pltpu.VMEM((8, length), F32),
            ],
        ),
        out_shape=jax.ShapeDtypeStruct((length, 3 * width), BF16),
        compiler_params=pltpu.CompilerParams(vmem_limit_bytes=48 * 2**20),
        cost_estimate=pl.CostEstimate(
            flops=20 * pairs * length * length * PAIR // 2,
            bytes_accessed=20 * length * width,
            transcendentals=pairs * length * length,
        ),
        name="attend_back",
    )(info, q_row, k_row, v_row, logs, attended, grads, cosine, sine)


def whole_pairs(values, kinds):
    own = values.shape[1] // kinds
    if own % PAIR == 0:
        return values
    values = jnp.pad(values.reshape(-1, kinds, own), ((0, 0), (0, 0), (0, PAIR - own % PAIR)))
    return values.reshape(values.shape[0], -1)


def own_heads(values, kinds, own):
    return values.reshape(values.shape[0], kinds, -1)[:, :, :own].reshape(values.shape[0], -1)


def rms_unit(values):
    factor = lax.rsqrt(jnp.mean(values * values, axis=-1, keepdims=True) + EPSILON)
    return (values * factor, factor)


def norm_back(grad_normed, unit_rows, factor, gain_row):
    scaled_grad = grad_normed * gain_row
    inner_mean = jnp.mean(scaled_grad * unit_rows, axis=-1, keepdims=True)
    return (
        factor * (scaled_grad - unit_rows * inner_mean),
        jnp.sum(grad_normed * unit_rows, axis=0),
    )


def row_layout(lengths, places):
    ends = [jnp.sum(lengths[: i + 1]) for i in range(lengths.shape[0])]
    begins = jnp.zeros_like(places)
    for end in ends:
        begins = jnp.where(places >= end, end, begins)
    return ends, places - begins


def rope_tables(within):
    half = HEAD_DIM // 2
    steps_up = jnp.arange(half, dtype=F32)
    frequency = ROPE_BASE ** (-2.0 * steps_up / HEAD_DIM)
    angles = within.astype(F32)[:, None] * frequency[None, :]
    cosine, sine = jnp.cos(angles), jnp.sin(angles)
    return (
        jnp.concatenate([cosine] * 4, axis=1),
        jnp.concatenate([-sine, sine, -sine, sine], axis=1),
    )


def body(
    tokens, doc_lengths, weight_qkv, weight_out, weight_gate_up, weight_down, norm_gains, cotangent
):
    sizes = [(axis, lax.axis_size(axis)) for axis in ("dp", "blk", "tensor")]
    size_dp, size_blk, size_tensor = (size for _, size in sizes)
    group = size_blk * size_tensor
    local_rows = tokens.shape[1]
    lengths = doc_lengths[0]

    me = (lax.axis_index("blk") * size_tensor + lax.axis_index("tensor")).astype(jnp.int32)
    order = jnp.array([*range(0, group, 2), *range(1, group, 2)], jnp.int32)
    places = (lax.bitwise_xor(order, me)[:, None] * local_rows) + jnp.arange(
        local_rows, dtype=jnp.int32
    )[None, :]
    ends, within = row_layout(lengths, places.reshape(-1))
    info = jnp.stack([me] + ends).astype(jnp.int32)
    cosine, sine = rope_tables(within)

    held_attention = named(
        "attention_weights", swap_columns, [weight_qkv, weight_out[:, None, :]], size_blk
    )
    full_attention = jnp.concatenate(held_attention, axis=1)
    full_attention = named("attention_gather", gather_rows, full_attention)
    cut = held_attention[0].shape[1]
    full_qkv, full_out = full_attention[:, :cut], full_attention[:, cut:]
    held_gate_up, held_down = named(
        "feed_weights",
        swap_columns,
        [after(weight_gate_up, *held_attention), weight_down[:, None, :]],
        size_blk,
    )
    gain_pair = named("gain_gather", gather_small, norm_gains, sizes)
    gain_first, gain_second = gain_pair[0], gain_pair[1]

    inputs = tokens[0].astype(F32)
    unit_first, factor_first = rms_unit(inputs)
    rows_first = (unit_first * gain_first).astype(BF16)
    rows_first, held_gate_up, held_down = together(rows_first, held_gate_up, held_down)
    normed_first, last_first = named("first_spread", spread, rows_first, PLANE, group)
    full_gate_up = named(
        "gate_up_gather", gather_rows, held_gate_up, full_attention, last_first
    )
    projected = dot_nn(normed_first, full_qkv)
    features = full_out.shape[1]
    attended, q_row, k_row, v_row, logs = attend(
        info, whole_pairs(projected, 3), cosine, sine, group
    )
    attended_here = own_heads(attended, 1, features)
    branch, _ = named(
        "branch_collect", collect, attended_here, full_out, dot_nt, PLANE, group
    )
    middle = inputs + branch
    unit_second, factor_second = rms_unit(middle)
    normed_second, _ = named("second_spread", spread, (unit_second * gain_second).astype(BF16), PLANE, group)
    hidden_here = full_gate_up.shape[1] // 2
    grad_output = cotangent[0].astype(F32)
    last_rows = cotangent[0]
    if normed_second.shape[0] > LONG_ROW:
        last_rows = after(last_rows, normed_second)
    grad_feed, _ = named("cotangent_spread", spread, last_rows, PLANE, group)
    full_down = named(
        "down_gather", gather_rows, held_down, full_gate_up, normed_second, grad_feed
    )
    gate = dot_nn(normed_second, full_gate_up[:, :hidden_here])
    up = dot_nn(normed_second, full_gate_up[:, hidden_here:])
    sigmoid_gate = jax.nn.sigmoid(gate)
    activated = gate * sigmoid_gate
    hidden = (activated * up).astype(BF16)
    grad_down = dot_tn(grad_feed, hidden).astype(BF16)
    wide = full_down.shape[1]
    full_down = after(full_down, grad_down)
    down_sum = named("down_back", sum_rows, after(grad_down, full_down))
    grad_hidden = dot_nn(grad_feed, full_down)
    silu_slope = sigmoid_gate * (1.0 + gate * (1.0 - sigmoid_gate))
    grad_gates = jnp.concatenate(
        [
            (grad_hidden * up * silu_slope).astype(BF16),
            (grad_hidden * activated).astype(BF16),
        ],
        axis=1,
    )
    grad_gate_up = dot_tn(normed_second, grad_gates).astype(BF16)
    grad_normed_second, last_second = named(
        "second_grad_collect", collect, grad_gates, full_gate_up, dot_nt, PLANE, group
    )
    grad_gate_up = after(grad_gate_up, down_sum, *last_second)
    gate_up_sum = named("gate_up_back", sum_rows, grad_gate_up)
    grad_middle_norm, sum_second = norm_back(
        grad_normed_second, unit_second, factor_second, gain_second
    )
    grad_middle = grad_output + grad_middle_norm
    grad_branch, _ = named("branch_grad_spread", spread, grad_middle.astype(BF16), PLANE, group)
    with jax.named_scope("feed_collect"):
        feed_hidden = after(hidden, *last_second)
        feed_out, _ = collect(
            feed_hidden, full_down, dot_nt, PLANE, group, begin=(grad_branch,)
        )
    [total_down] = named(
        "down_return", return_columns, after(down_sum, grad_branch), size_blk, [1], wide
    )
    grad_out = dot_tn(grad_branch, attended_here).astype(BF16)
    grad_attended = dot_nn(grad_branch, full_out).astype(BF16)
    grad_projected = attend_back(
        info,
        q_row,
        k_row,
        v_row,
        logs,
        attended,
        whole_pairs(grad_attended, 1),
        cosine,
        sine,
        group,
    )
    grad_projected = own_heads(grad_projected, 3, features)
    grad_qkv = dot_tn(normed_first, grad_projected).astype(BF16)
    grad_normed_first, last_grad = named(
        "first_grad_collect", collect, grad_projected, full_qkv, dot_nt, PLANE, group
    )
    both = jnp.concatenate([grad_qkv, grad_out], axis=1)
    both_sum = named("attention_back", sum_rows, after(both, gate_up_sum, feed_out, total_down, *last_grad))

    outcome = (middle + feed_out).astype(BF16)
    grad_input_norm, sum_first = norm_back(grad_normed_first, unit_first, factor_first, gain_first)
    grad_input = grad_middle + grad_input_norm
    gain_sums = named("gain_scatter", scatter_small, jnp.stack([sum_first, sum_second]), sizes)
    [total_gate_up] = named(
        "gate_up_return", return_columns, gate_up_sum, size_blk, [2], wide
    )
    both_sum = after(both_sum, total_gate_up, outcome, grad_input, gain_sums)
    total_qkv, total_out = named(
        "attention_return", return_columns, both_sum, size_blk, [3, 1], features
    )
    return (
        outcome[None],
        grad_input[None],
        total_qkv,
        total_out[:, 0],
        total_gate_up,
        total_down[:, 0],
        gain_sums,
    )


def solution(mesh):
    return jax.shard_map(
        body,
        mesh=mesh,
        in_specs=(
            P("dp", ("blk", "tensor"), None),
            P("dp", None),
            P(("dp", "blk"), None, "tensor"),
            P(("dp", "blk"), "tensor"),
            P(("dp", "blk"), None, "tensor"),
            P(("dp", "blk"), "tensor"),
            P(None, ("dp", "blk", "tensor")),
            P("dp", ("blk", "tensor"), None),
        ),
        out_specs=(
            P("dp", ("blk", "tensor"), None),
            P("dp", ("blk", "tensor"), None),
            P(("dp", "blk"), None, "tensor"),
            P(("dp", "blk"), "tensor"),
            P(("dp", "blk"), None, "tensor"),
            P(("dp", "blk"), "tensor"),
            P(None, ("dp", "blk", "tensor")),
        ),
        check_vma=False,
    )
```

```python
import functools

import jax
import jax.numpy as jnp
from jax import lax
from jax.experimental import pallas as pl
from jax.experimental.pallas import tpu as pltpu
from jax.sharding import PartitionSpec as P

HEAD_DIM = 64
PAIR = 2 * HEAD_DIM
EPSILON = 1e-05
ROPE_BASE = 130000.0
NEGATIVE = -1e30
QUERY_BLOCK = 256
UNROLLED = 4
LONG_ROW = 2048
PLANE = ("blk", "tensor")
F32 = jnp.float32
BF16 = jnp.bfloat16


def dot_nn(a, b):
    return lax.dot_general(a, b, (((1,), (0,)), ((), ())), preferred_element_type=F32)


def dot_nt(a, b):
    return lax.dot_general(a, b, (((1,), (1,)), ((), ())), preferred_element_type=F32)


def dot_tn(a, b):
    return lax.dot_general(a, b, (((0,), (0,)), ((), ())), preferred_element_type=F32)


def named(name, function, *args):
    with jax.named_scope(name):
        return function(*args)


def after(value, *events):
    return lax.optimization_barrier((value, *events))[0]


def together(*values):
    return lax.optimization_barrier(values)


def swap_by(value, axes, size, bits):
    return lax.ppermute(value, axes, [(i, i ^ bits) for i in range(size)])


def join_kernel(steps, near_ref, far_ref, out_ref):
    step = pl.program_id(0)

    @pl.when(step < steps)
    def _():
        out_ref[...] = near_ref[...]

    @pl.when(step >= steps)
    def _():
        out_ref[...] = far_ref[...]


def join_halves(near, far):
    rows, width = near.shape
    steps = max(1, rows // 128)
    block = (rows // steps, width)
    return pl.pallas_call(
        functools.partial(join_kernel, steps),
        grid=(2 * steps,),
        in_specs=[
            pl.BlockSpec(block, lambda i: (jnp.minimum(i, steps - 1), 0)),
            pl.BlockSpec(block, lambda i: (jnp.maximum(i - steps, 0), 0)),
        ],
        out_specs=pl.BlockSpec(block, lambda i: (i, 0)),
        out_shape=jax.ShapeDtypeStruct((2 * rows, width), near.dtype),
        cost_estimate=pl.CostEstimate(
            flops=0, bytes_accessed=8 * rows * width, transcendentals=0
        ),
        name="join_halves",
    )(near, far)


def spread(rows, axes, size):
    pieces = [swap_by(rows, axes, size, bits) for bits in range(2, size, 2)]
    near = jnp.concatenate([rows] + pieces, axis=0)
    return join_halves(near, swap_by(near, axes, size, 1)), pieces[-1]


def collect(left, right, product, axes, size, begin=()):
    half = left.shape[0] // 2
    received = swap_by(product(left[half:], right).astype(BF16), axes, size, 1)
    near = (product(left[:half], right) + received.astype(F32)).astype(BF16)
    if begin:
        near = after(near, *begin)
    rows = near.shape[0] // (size // 2)
    blocks = [
        swap_by(near[place * rows : (place + 1) * rows], axes, size, 2 * place)
        for place in range(1, size // 2)
    ]
    summed = sum([block.astype(F32) for block in blocks], near[:rows].astype(F32))
    return summed, blocks


def gather_small(value, axis_sizes):
    for axis, size in reversed(axis_sizes):
        index = lax.axis_index(axis)
        bit = 1
        while bit < size:
            other = swap_by(value, axis, size, bit)
            low = (index & bit) == 0
            value = jnp.concatenate(
                [jnp.where(low, value, other), jnp.where(low, other, value)], axis=1
            )
            bit *= 2
    return value


def scatter_small(value, axis_sizes):
    sizes = [size for _, size in axis_sizes]
    kinds = value.shape[0]
    value = value.reshape(kinds, sizes[0], -1).swapaxes(1, 2).reshape(kinds, *sizes[1:], -1)
    value = value.reshape(kinds, -1, value.shape[-1] // sizes[0], sizes[0])
    value = value.swapaxes(2, 3).reshape(kinds, -1)
    for axis, size in (*axis_sizes[1:], axis_sizes[0]):
        index = lax.axis_index(axis)
        bit = size // 2
        while bit >= 1:
            half = value.shape[1] // 2
            low = (index & bit) == 0
            kept = jnp.where(low, value[:, :half], value[:, half:])
            sent = jnp.where(low, value[:, half:], value[:, :half])
            value = kept + swap_by(sent, axis, size, bit)
            bit //= 2
    return value


def trade(blocks, axis):
    return lax.all_to_all(blocks, axis, 0, 0, tiled=True)


def split_columns(weight, blocks):
    rows, kinds, columns = weight.shape
    parted = weight.reshape(rows, kinds, blocks, columns // blocks).transpose(2, 0, 1, 3)
    return parted.reshape(blocks, rows, -1)


def swap_columns(weights, blocks):
    parts = [split_columns(weight, blocks) for weight in weights]
    traded = trade(jnp.concatenate(parts, axis=2), "blk")
    traded = traded.reshape(-1, traded.shape[2])
    cuts = []
    start = 0
    for part in parts:
        cuts.append(traded[:, start : start + part.shape[2]])
        start += part.shape[2]
    return cuts


def gather_rows(weight, *events):
    return lax.all_gather(after(weight, *events), "dp", axis=0, tiled=True)


def sum_rows(grads):
    return lax.psum_scatter(grads, "dp", scatter_dimension=0, tiled=True)


def own_then_other(blocks):
    first = lax.axis_index("blk") == 0
    return jnp.where(first, blocks[0], blocks[1]), jnp.where(first, blocks[1], blocks[0])


def trade_rows(grads, size_dp):
    split = grads.reshape(size_dp, 2, -1, grads.shape[1])
    own, sent = own_then_other([split[:, 0], split[:, 1]])
    return [part.reshape(-1, grads.shape[1]) for part in (own, swap_by(sent, "blk", 2, 1))]


def join_columns(parted, kinds, wide):
    totals = []
    start = 0
    for kind in kinds:
        columns = [
            [part[:, start + i * wide : start + (i + 1) * wide] for part in parted]
            for i in range(kind)
        ]
        totals.append(jnp.stack([jnp.concatenate(part, axis=1) for part in columns], axis=1))
        start += kind * wide
    return totals


def return_columns(summed, blocks, kinds, wide):
    parted = summed.reshape(blocks, -1, summed.shape[1])
    if blocks == 2:
        own, sent = own_then_other(parted)
        got = swap_by(sent, "blk", blocks, 1)
        parted = own_then_other([own.astype(F32), got.astype(F32)])
    else:
        parted = list(trade(parted, "blk").astype(F32))
    return join_columns(parted, kinds, wide)


def swap_halves(values):
    lane = lax.broadcasted_iota(jnp.int32, values.shape, 1)
    half = HEAD_DIM // 2
    return jnp.where(
        lane % HEAD_DIM < half,
        pltpu.roll(values, PAIR - half, 1),
        pltpu.roll(values, half, 1),
    )


def relative_place(block, info_ref, blocks, rows):
    bits = lax.bitwise_xor(jnp.int32(block), info_ref[0])
    place = lax.shift_right_logical(bits, 1) + (bits & 1) * (blocks // 2)
    return pl.ds(pl.multiple_of(place * rows, rows), rows)


def document_start(places, info_ref):
    end_0 = info_ref[1]
    end_1 = info_ref[2]
    end_2 = info_ref[3]
    start = jnp.where(places >= end_0, end_0, 0)
    start = jnp.where(places >= end_1, end_1, start)
    return jnp.where(places >= end_2, end_2, start)


def head_lanes(shape, head):
    lane = lax.broadcasted_iota(jnp.int32, shape, 1)
    return (lane < HEAD_DIM) if head == 0 else (lane >= HEAD_DIM)


def only_head(values, head):
    return jnp.where(head_lanes(values.shape, head), values, jnp.zeros_like(values))


def attend_kernel(
    blocks,
    info_ref,
    q_ref,
    k_ref,
    v_ref,
    cos_ref,
    sin_ref,
    out_ref,
    q_row,
    k_row,
    v_row,
    log_ref,
):
    length = q_ref.shape[0]
    rows = length // blocks
    score_scale = HEAD_DIM ** (-0.5)
    for block in range(blocks):
        here = relative_place(block, info_ref, blocks, rows)
        there = pl.ds(block * rows, rows)
        cosine, sine = cos_ref[here, :], sin_ref[here, :]
        q, k = q_ref[here, :], k_ref[here, :]
        q_row[there, :] = ((q * cosine + swap_halves(q) * sine) * score_scale).astype(BF16)
        k_row[there, :] = (k * cosine + swap_halves(k) * sine).astype(BF16)
        v_row[there, :] = v_ref[here, :].astype(BF16)

    tall = max(QUERY_BLOCK, rows)

    def query_step(first, width):
        queries = q_row[pl.ds(first, tall), :]
        places = first + lax.broadcasted_iota(jnp.int32, (tall, 1), 0)
        keys_at = lax.broadcasted_iota(jnp.int32, (tall, width), 1)
        allowed = (keys_at <= places) & (keys_at >= document_start(places, info_ref))
        results = []
        logs = []
        for head in range(2):
            scores = dot_nt(only_head(queries, head), k_row[:width, :])
            scores = jnp.where(allowed, scores, NEGATIVE)
            highest = jnp.max(scores, axis=1, keepdims=True)
            weights = jnp.exp(scores - highest)
            total = jnp.sum(weights, axis=1, keepdims=True)
            results.append(dot_nn(weights.astype(BF16), v_row[:width, :]) / total)
            logs.append(highest + jnp.log(total))
        first_head = head_lanes((tall, PAIR), 0)
        present = (places < info_ref[3]).astype(F32)
        merged = (jnp.where(first_head, results[0], results[1]) * present).astype(BF16)
        log_ref[pl.ds(first, tall), :] = jnp.where(first_head, logs[0], logs[1])
        return merged

    def put(merged, first_block):
        for part in range(tall // rows):
            here = relative_place(first_block + part, info_ref, blocks, rows)
            out_ref[here, :] = merged[part * rows : (part + 1) * rows]

    steps = length // tall
    if steps <= UNROLLED:
        for step in range(steps):
            put(query_step(step * tall, (step + 1) * tall), step * (tall // rows))
    else:

        @pl.loop(0, steps)
        def _(step):
            put(query_step(pl.multiple_of(step * tall, tall), length), step * (tall // rows))


def attend(info, projected, cosine, sine, blocks):
    length, width = projected.shape
    pairs = width // 3 // PAIR
    whole = lambda kind: pl.BlockSpec((length, PAIR), lambda p, _: (0, kind * pairs + p))
    table = pl.BlockSpec((length, PAIR), lambda p, _: (0, 0))
    shape = lambda kind: jax.ShapeDtypeStruct((length, pairs * PAIR), kind)
    return pl.pallas_call(
        functools.partial(attend_kernel, blocks),
        grid_spec=pltpu.PrefetchScalarGridSpec(
            num_scalar_prefetch=1,
            grid=(pairs,),
            in_specs=[whole(0), whole(1), whole(2), table, table],
            out_specs=[whole(0)] * 5,
        ),
        out_shape=[shape(BF16), shape(BF16), shape(BF16), shape(BF16), shape(F32)],
        compiler_params=pltpu.CompilerParams(vmem_limit_bytes=48 * 2**20),
        cost_estimate=pl.CostEstimate(
            flops=8 * pairs * length * length * PAIR // 2,
            bytes_accessed=6 * length * width,
            transcendentals=pairs * length * length,
        ),
        name="attend",
    )(info, projected, projected, projected, cosine, sine)


def attend_back_kernel(
    blocks,
    info_ref,
    q_row,
    k_row,
    v_row,
    log_ref,
    out_ref,
    grad_ref,
    cos_ref,
    sin_ref,
    back_ref,
    g_row,
    q_sum,
    k_sum,
    v_sum,
    log_flat,
    inner_flat,
):
    length = q_row.shape[0]
    rows = length // blocks
    score_scale = HEAD_DIM ** (-0.5)
    kind = pl.program_id(1)
    tall = max(QUERY_BLOCK, rows)

    @pl.when(kind == 0)
    def _():
        for block in range(blocks):
            here = relative_place(block, info_ref, blocks, rows)
            there = pl.ds(block * rows, rows)
            places = block * rows + lax.broadcasted_iota(jnp.int32, (rows, 1), 0)
            present = (places < info_ref[3]).astype(F32)
            grads = grad_ref[here, :].astype(F32) * present
            g_row[there, :] = grads.astype(BF16)
            inner = (grads * out_ref[here, :].astype(F32)).T
            for head in range(2):
                span = slice(head * HEAD_DIM, (head + 1) * HEAD_DIM)
                inner_flat[head : head + 1, there] = jnp.sum(inner[span], axis=0, keepdims=True)
            logs = log_ref[there, :].T
            for head in range(2):
                log_flat[head : head + 1, there] = logs[head * HEAD_DIM : head * HEAD_DIM + 1]
        q_sum[...] = jnp.zeros_like(q_sum)

        def key_step(first, from_query):
            width = length - from_query
            span = slice(from_query, length)
            keys = k_row[pl.ds(first, tall), :]
            values = v_row[pl.ds(first, tall), :]
            keys_at = first + lax.broadcasted_iota(jnp.int32, (tall, 1), 0)
            places = from_query + lax.broadcasted_iota(jnp.int32, (1, width), 1)
            allowed = (keys_at <= places) & (keys_at >= document_start(places, info_ref))
            queries, grads = q_row[span, :], g_row[span, :]
            k_parts = []
            v_parts = []
            for head in range(2):
                keys_head = only_head(keys, head)
                scores = dot_nt(keys_head, queries)
                raised = jnp.exp(scores - log_flat[head : head + 1, span])
                weights = jnp.where(allowed, raised, 0.0)
                grad_weights = dot_nt(only_head(values, head), grads)
                grad_scores = weights * (grad_weights - inner_flat[head : head + 1, span])
                grad_scores = grad_scores.astype(BF16)
                v_parts.append(dot_nn(weights.astype(BF16), grads))
                k_parts.append(dot_nn(grad_scores, queries))
                q_sum[span, :] += dot_tn(grad_scores, keys_head)
            first_head = head_lanes((tall, PAIR), 0)
            k_sum[pl.ds(first, tall), :] = jnp.where(first_head, k_parts[0], k_parts[1])
            v_sum[pl.ds(first, tall), :] = jnp.where(first_head, v_parts[0], v_parts[1])

        steps = length // tall
        if steps <= UNROLLED:
            for step in range(steps):
                key_step(step * tall, step * tall)
        else:

            @pl.loop(0, steps)
            def _(step):
                key_step(pl.multiple_of(step * tall, tall), 0)

    def give(source, turned, scale):
        for block in range(blocks):
            here = relative_place(block, info_ref, blocks, rows)
            grads = source[pl.ds(block * rows, rows), :] * scale
            if turned:
                grads = grads * cos_ref[here, :] - swap_halves(grads) * sin_ref[here, :]
            back_ref[here, :] = grads.astype(BF16)

    pl.when(kind == 0)(lambda: give(q_sum, True, score_scale))
    pl.when(kind == 1)(lambda: give(k_sum, True, 1.0))
    pl.when(kind == 2)(lambda: give(v_sum, False, 1.0))


def attend_back(info, q_row, k_row, v_row, logs, attended, grads, cosine, sine, blocks):
    length, width = q_row.shape
    pairs = width // PAIR
    one = pl.BlockSpec((length, PAIR), lambda p, c, _: (0, p))
    table = pl.BlockSpec((length, PAIR), lambda p, c, _: (0, 0))
    return pl.pallas_call(
        functools.partial(attend_back_kernel, blocks),
        grid_spec=pltpu.PrefetchScalarGridSpec(
            num_scalar_prefetch=1,
            grid=(pairs, 3),
            in_specs=[one] * 6 + [table] * 2,
            out_specs=pl.BlockSpec((length, PAIR), lambda p, c, _: (0, c * pairs + p)),
            scratch_shapes=[
                pltpu.VMEM((length, PAIR), BF16),
                pltpu.VMEM((length, PAIR), F32),
                pltpu.VMEM((length, PAIR), F32),
                pltpu.VMEM((length, PAIR), F32),
                pltpu.VMEM((8, length), F32),
                pltpu.VMEM((8, length), F32),
            ],
        ),
        out_shape=jax.ShapeDtypeStruct((length, 3 * width), BF16),
        compiler_params=pltpu.CompilerParams(vmem_limit_bytes=48 * 2**20),
        cost_estimate=pl.CostEstimate(
            flops=20 * pairs * length * length * PAIR // 2,
            bytes_accessed=20 * length * width,
            transcendentals=pairs * length * length,
        ),
        name="attend_back",
    )(info, q_row, k_row, v_row, logs, attended, grads, cosine, sine)


def whole_pairs(values, kinds):
    own = values.shape[1] // kinds
    if own % PAIR == 0:
        return values
    values = jnp.pad(values.reshape(-1, kinds, own), ((0, 0), (0, 0), (0, PAIR - own % PAIR)))
    return values.reshape(values.shape[0], -1)


def own_heads(values, kinds, own):
    return values.reshape(values.shape[0], kinds, -1)[:, :, :own].reshape(values.shape[0], -1)


def rms_unit(values):
    factor = lax.rsqrt(jnp.mean(values * values, axis=-1, keepdims=True) + EPSILON)
    return (values * factor, factor)


def norm_back(grad_normed, unit_rows, factor, gain_row):
    scaled_grad = grad_normed * gain_row
    inner_mean = jnp.mean(scaled_grad * unit_rows, axis=-1, keepdims=True)
    return (
        factor * (scaled_grad - unit_rows * inner_mean),
        jnp.sum(grad_normed * unit_rows, axis=0),
    )


def row_layout(lengths, places):
    ends = [jnp.sum(lengths[: i + 1]) for i in range(lengths.shape[0])]
    begins = jnp.zeros_like(places)
    for end in ends:
        begins = jnp.where(places >= end, end, begins)
    return ends, places - begins


def rope_tables(within):
    half = HEAD_DIM // 2
    steps_up = jnp.arange(half, dtype=F32)
    frequency = ROPE_BASE ** (-2.0 * steps_up / HEAD_DIM)
    angles = within.astype(F32)[:, None] * frequency[None, :]
    cosine, sine = jnp.cos(angles), jnp.sin(angles)
    return (
        jnp.concatenate([cosine] * 4, axis=1),
        jnp.concatenate([-sine, sine, -sine, sine], axis=1),
    )


def body(
    tokens, doc_lengths, weight_qkv, weight_out, weight_gate_up, weight_down, norm_gains, cotangent
):
    sizes = [(axis, lax.axis_size(axis)) for axis in ("dp", "blk", "tensor")]
    size_dp, size_blk, size_tensor = (size for _, size in sizes)
    group = size_blk * size_tensor
    local_rows = tokens.shape[1]
    lengths = doc_lengths[0]

    me = (lax.axis_index("blk") * size_tensor + lax.axis_index("tensor")).astype(jnp.int32)
    order = jnp.array([*range(0, group, 2), *range(1, group, 2)], jnp.int32)
    places = (lax.bitwise_xor(order, me)[:, None] * local_rows) + jnp.arange(
        local_rows, dtype=jnp.int32
    )[None, :]
    ends, within = row_layout(lengths, places.reshape(-1))
    info = jnp.stack([me] + ends).astype(jnp.int32)
    cosine, sine = rope_tables(within)

    held_attention = named(
        "attention_weights", swap_columns, [weight_qkv, weight_out[:, None, :]], size_blk
    )
    full_attention = jnp.concatenate(held_attention, axis=1)
    full_attention = named("attention_gather", gather_rows, full_attention)
    cut = held_attention[0].shape[1]
    full_qkv, full_out = full_attention[:, :cut], full_attention[:, cut:]
    held_gate_up, held_down = named(
        "feed_weights",
        swap_columns,
        [after(weight_gate_up, *held_attention), weight_down[:, None, :]],
        size_blk,
    )
    gain_pair = named("gain_gather", gather_small, norm_gains, sizes)
    gain_first, gain_second = gain_pair[0], gain_pair[1]

    inputs = tokens[0].astype(F32)
    unit_first, factor_first = rms_unit(inputs)
    rows_first = (unit_first * gain_first).astype(BF16)
    rows_first, held_gate_up, held_down = together(rows_first, held_gate_up, held_down)
    normed_first, last_first = named("first_spread", spread, rows_first, PLANE, group)
    full_gate_up = named(
        "gate_up_gather", gather_rows, held_gate_up, full_attention, last_first
    )
    projected = dot_nn(normed_first, full_qkv)
    features = full_out.shape[1]
    attended, q_row, k_row, v_row, logs = attend(
        info, whole_pairs(projected, 3), cosine, sine, group
    )
    attended_here = own_heads(attended, 1, features)
    branch, _ = named(
        "branch_collect", collect, attended_here, full_out, dot_nt, PLANE, group
    )
    middle = inputs + branch
    unit_second, factor_second = rms_unit(middle)
    normed_second, _ = named("second_spread", spread, (unit_second * gain_second).astype(BF16), PLANE, group)
    hidden_here = full_gate_up.shape[1] // 2
    grad_output = cotangent[0].astype(F32)
    last_rows = cotangent[0]
    if normed_second.shape[0] > LONG_ROW:
        last_rows = after(last_rows, normed_second)
    grad_feed, _ = named("cotangent_spread", spread, last_rows, PLANE, group)
    full_down = named(
        "down_gather", gather_rows, held_down, full_gate_up, normed_second, grad_feed
    )
    gate = dot_nn(normed_second, full_gate_up[:, :hidden_here])
    up = dot_nn(normed_second, full_gate_up[:, hidden_here:])
    sigmoid_gate = jax.nn.sigmoid(gate)
    activated = gate * sigmoid_gate
    hidden = (activated * up).astype(BF16)
    grad_down = dot_tn(grad_feed, hidden).astype(BF16)
    wide = full_down.shape[1]
    full_down = after(full_down, grad_down)
    down_sum = named("down_back", sum_rows, after(grad_down, full_down))
    grad_hidden = dot_nn(grad_feed, full_down)
    silu_slope = sigmoid_gate * (1.0 + gate * (1.0 - sigmoid_gate))
    grad_gates = jnp.concatenate(
        [
            (grad_hidden * up * silu_slope).astype(BF16),
            (grad_hidden * activated).astype(BF16),
        ],
        axis=1,
    )
    grad_gate_up = dot_tn(normed_second, grad_gates).astype(BF16)
    grad_normed_second, last_second = named(
        "second_grad_collect", collect, grad_gates, full_gate_up, dot_nt, PLANE, group
    )
    grad_gate_up = after(grad_gate_up, down_sum, *last_second)
    gate_up_sum = named("gate_up_back", sum_rows, grad_gate_up)
    grad_middle_norm, sum_second = norm_back(
        grad_normed_second, unit_second, factor_second, gain_second
    )
    grad_middle = grad_output + grad_middle_norm
    grad_branch, _ = named("branch_grad_spread", spread, grad_middle.astype(BF16), PLANE, group)
    [total_down] = named(
        "down_return", return_columns, after(down_sum, grad_branch), size_blk, [1], wide
    )
    grad_out = dot_tn(grad_branch, attended_here).astype(BF16)
    grad_attended = dot_nn(grad_branch, full_out).astype(BF16)
    if size_blk == 2:
        out_parts = named("out_trade", trade_rows, grad_out, size_dp)
    grad_projected = attend_back(
        info,
        q_row,
        k_row,
        v_row,
        logs,
        attended,
        whole_pairs(grad_attended, 1),
        cosine,
        sine,
        group,
    )
    grad_projected = own_heads(grad_projected, 3, features)
    if size_blk == 2:
        grad_projected, *out_parts = together(grad_projected, *out_parts)
        grad_qkv = dot_tn(normed_first, grad_projected).astype(BF16)
        qkv_parts = named("qkv_trade", trade_rows, grad_qkv, size_dp)
        parts = [qkv_parts[0], out_parts[0], qkv_parts[1], out_parts[1]]
    else:
        parts = [dot_tn(normed_first, grad_projected).astype(BF16), grad_out]
    grad_normed_first, last_grad = named(
        "first_grad_collect", collect, grad_projected, full_qkv, dot_nt, PLANE, group
    )
    both = after(jnp.concatenate(parts, axis=1), gate_up_sum, *last_grad)
    both_sum = named("attention_back", sum_rows, both)
    with jax.named_scope("feed_collect"):
        feed_hidden = after(hidden, *last_second)
        feed_out, _ = collect(
            feed_hidden, full_down, dot_nt, PLANE, group, begin=last_grad
        )
    outcome = (middle + feed_out).astype(BF16)
    grad_input_norm, sum_first = norm_back(grad_normed_first, unit_first, factor_first, gain_first)
    grad_input = grad_middle + grad_input_norm
    gain_sums = named("gain_scatter", scatter_small, jnp.stack([sum_first, sum_second]), sizes)
    [total_gate_up] = named(
        "gate_up_return", return_columns, gate_up_sum, size_blk, [2], wide
    )
    both_sum = after(both_sum, total_gate_up, total_down, outcome, grad_input, gain_sums)
    if size_blk == 2:
        half = both_sum.shape[1] // 2
        summed = both_sum.astype(F32)
        parted = own_then_other([summed[:, :half], summed[:, half:]])
        total_qkv, total_out = join_columns(parted, [3, 1], features)
    else:
        total_qkv, total_out = return_columns(both_sum, size_blk, [3, 1], features)
    return (
        outcome[None],
        grad_input[None],
        total_qkv,
        total_out[:, 0],
        total_gate_up,
        total_down[:, 0],
        gain_sums,
    )


def solution(mesh):
    return jax.shard_map(
        body,
        mesh=mesh,
        in_specs=(
            P("dp", ("blk", "tensor"), None),
            P("dp", None),
            P(("dp", "blk"), None, "tensor"),
            P(("dp", "blk"), "tensor"),
            P(("dp", "blk"), None, "tensor"),
            P(("dp", "blk"), "tensor"),
            P(None, ("dp", "blk", "tensor")),
            P("dp", ("blk", "tensor"), None),
        ),
        out_specs=(
            P("dp", ("blk", "tensor"), None),
            P("dp", ("blk", "tensor"), None),
            P(("dp", "blk"), None, "tensor"),
            P(("dp", "blk"), "tensor"),
            P(("dp", "blk"), None, "tensor"),
            P(("dp", "blk"), "tensor"),
            P(None, ("dp", "blk", "tensor")),
        ),
        check_vma=False,
    )
```

```python
import functools

import jax
import jax.numpy as jnp
from jax import lax
from jax.experimental import pallas as pl
from jax.experimental.pallas import tpu as pltpu
from jax.sharding import PartitionSpec as P

HEAD_DIM = 64
PAIR = 2 * HEAD_DIM
EPSILON = 1e-05
ROPE_BASE = 130000.0
NEGATIVE = -1e30
QUERY_BLOCK = 256
UNROLLED = 4
LONG_ROW = 2048
PLANE = ("blk", "tensor")
F32 = jnp.float32
BF16 = jnp.bfloat16


def dot_nn(a, b):
    return lax.dot_general(a, b, (((1,), (0,)), ((), ())), preferred_element_type=F32)


def dot_nt(a, b):
    return lax.dot_general(a, b, (((1,), (1,)), ((), ())), preferred_element_type=F32)


def dot_tn(a, b):
    return lax.dot_general(a, b, (((0,), (0,)), ((), ())), preferred_element_type=F32)


def named(name, function, *args):
    with jax.named_scope(name):
        return function(*args)


def after(value, *events):
    return lax.optimization_barrier((value, *events))[0]


def together(*values):
    return lax.optimization_barrier(values)


def swap_by(value, axes, size, bits):
    return lax.ppermute(value, axes, [(i, i ^ bits) for i in range(size)])


def join_kernel(steps, near_ref, far_ref, out_ref):
    step = pl.program_id(0)

    @pl.when(step < steps)
    def _():
        out_ref[...] = near_ref[...]

    @pl.when(step >= steps)
    def _():
        out_ref[...] = far_ref[...]


def join_halves(near, far):
    rows, width = near.shape
    steps = max(1, rows // 128)
    block = (rows // steps, width)
    return pl.pallas_call(
        functools.partial(join_kernel, steps),
        grid=(2 * steps,),
        in_specs=[
            pl.BlockSpec(block, lambda i: (jnp.minimum(i, steps - 1), 0)),
            pl.BlockSpec(block, lambda i: (jnp.maximum(i - steps, 0), 0)),
        ],
        out_specs=pl.BlockSpec(block, lambda i: (i, 0)),
        out_shape=jax.ShapeDtypeStruct((2 * rows, width), near.dtype),
        cost_estimate=pl.CostEstimate(
            flops=0, bytes_accessed=8 * rows * width, transcendentals=0
        ),
        name="join_halves",
    )(near, far)


def spread(rows, axes, size):
    pieces = [swap_by(rows, axes, size, bits) for bits in range(2, size, 2)]
    near = jnp.concatenate([rows] + pieces, axis=0)
    return join_halves(near, swap_by(near, axes, size, 1)), pieces[-1]


def collect(left, right, product, axes, size, begin=()):
    half = left.shape[0] // 2
    received = swap_by(product(left[half:], right).astype(BF16), axes, size, 1)
    near = (product(left[:half], right) + received.astype(F32)).astype(BF16)
    if begin:
        near = after(near, *begin)
    rows = near.shape[0] // (size // 2)
    blocks = [
        swap_by(near[place * rows : (place + 1) * rows], axes, size, 2 * place)
        for place in range(1, size // 2)
    ]
    summed = sum([block.astype(F32) for block in blocks], near[:rows].astype(F32))
    return summed, blocks


def gather_small(value, axis_sizes):
    for axis, size in reversed(axis_sizes):
        index = lax.axis_index(axis)
        bit = 1
        while bit < size:
            other = swap_by(value, axis, size, bit)
            low = (index & bit) == 0
            value = jnp.concatenate(
                [jnp.where(low, value, other), jnp.where(low, other, value)], axis=1
            )
            bit *= 2
    return value


def scatter_small(value, axis_sizes):
    sizes = [size for _, size in axis_sizes]
    kinds = value.shape[0]
    value = value.reshape(kinds, sizes[0], -1).swapaxes(1, 2).reshape(kinds, *sizes[1:], -1)
    value = value.reshape(kinds, -1, value.shape[-1] // sizes[0], sizes[0])
    value = value.swapaxes(2, 3).reshape(kinds, -1)
    for axis, size in (*axis_sizes[1:], axis_sizes[0]):
        index = lax.axis_index(axis)
        bit = size // 2
        while bit >= 1:
            half = value.shape[1] // 2
            low = (index & bit) == 0
            kept = jnp.where(low, value[:, :half], value[:, half:])
            sent = jnp.where(low, value[:, half:], value[:, :half])
            value = kept + swap_by(sent, axis, size, bit)
            bit //= 2
    return value


def trade(blocks, axis):
    return lax.all_to_all(blocks, axis, 0, 0, tiled=True)


def split_columns(weight, blocks):
    rows, kinds, columns = weight.shape
    parted = weight.reshape(rows, kinds, blocks, columns // blocks).transpose(2, 0, 1, 3)
    return parted.reshape(blocks, rows, -1)


def swap_columns(weights, blocks):
    parts = [split_columns(weight, blocks) for weight in weights]
    traded = trade(jnp.concatenate(parts, axis=2), "blk")
    traded = traded.reshape(-1, traded.shape[2])
    cuts = []
    start = 0
    for part in parts:
        cuts.append(traded[:, start : start + part.shape[2]])
        start += part.shape[2]
    return cuts


def gather_rows(weight, *events):
    return lax.all_gather(after(weight, *events), "dp", axis=0, tiled=True)


def sum_rows(grads):
    return lax.psum_scatter(grads, "dp", scatter_dimension=0, tiled=True)


def own_then_other(blocks):
    first = lax.axis_index("blk") == 0
    return jnp.where(first, blocks[0], blocks[1]), jnp.where(first, blocks[1], blocks[0])


def trade_rows(grads, size_dp):
    split = grads.reshape(size_dp, 2, -1, grads.shape[1])
    own, sent = own_then_other([split[:, 0], split[:, 1]])
    return [part.reshape(-1, grads.shape[1]) for part in (own, swap_by(sent, "blk", 2, 1))]


def join_rows(own, sent, size_dp):
    parts = own_then_other([own, swap_by(sent, "blk", 2, 1)])
    parts = [part.reshape(size_dp, -1, own.shape[1]) for part in parts]
    return jnp.stack(parts, axis=1).reshape(-1, own.shape[1])


def join_columns(parted, kinds, wide):
    totals = []
    start = 0
    for kind in kinds:
        columns = [
            [part[:, start + i * wide : start + (i + 1) * wide] for part in parted]
            for i in range(kind)
        ]
        totals.append(jnp.stack([jnp.concatenate(part, axis=1) for part in columns], axis=1))
        start += kind * wide
    return totals


def return_columns(summed, blocks, kinds, wide):
    parted = summed.reshape(blocks, -1, summed.shape[1])
    if blocks == 2:
        own, sent = own_then_other(parted)
        got = swap_by(sent, "blk", blocks, 1)
        parted = own_then_other([own.astype(F32), got.astype(F32)])
    else:
        parted = list(trade(parted, "blk").astype(F32))
    return join_columns(parted, kinds, wide)


def swap_halves(values):
    lane = lax.broadcasted_iota(jnp.int32, values.shape, 1)
    half = HEAD_DIM // 2
    return jnp.where(
        lane % HEAD_DIM < half,
        pltpu.roll(values, PAIR - half, 1),
        pltpu.roll(values, half, 1),
    )


def relative_place(block, info_ref, blocks, rows):
    bits = lax.bitwise_xor(jnp.int32(block), info_ref[0])
    place = lax.shift_right_logical(bits, 1) + (bits & 1) * (blocks // 2)
    return pl.ds(pl.multiple_of(place * rows, rows), rows)


def document_start(places, info_ref):
    end_0 = info_ref[1]
    end_1 = info_ref[2]
    end_2 = info_ref[3]
    start = jnp.where(places >= end_0, end_0, 0)
    start = jnp.where(places >= end_1, end_1, start)
    return jnp.where(places >= end_2, end_2, start)


def head_lanes(shape, head):
    lane = lax.broadcasted_iota(jnp.int32, shape, 1)
    return (lane < HEAD_DIM) if head == 0 else (lane >= HEAD_DIM)


def only_head(values, head):
    return jnp.where(head_lanes(values.shape, head), values, jnp.zeros_like(values))


def attend_kernel(
    blocks,
    info_ref,
    q_ref,
    k_ref,
    v_ref,
    cos_ref,
    sin_ref,
    out_ref,
    q_row,
    k_row,
    v_row,
    log_ref,
):
    length = q_ref.shape[0]
    rows = length // blocks
    score_scale = HEAD_DIM ** (-0.5)
    for block in range(blocks):
        here = relative_place(block, info_ref, blocks, rows)
        there = pl.ds(block * rows, rows)
        cosine, sine = cos_ref[here, :], sin_ref[here, :]
        q, k = q_ref[here, :], k_ref[here, :]
        q_row[there, :] = ((q * cosine + swap_halves(q) * sine) * score_scale).astype(BF16)
        k_row[there, :] = (k * cosine + swap_halves(k) * sine).astype(BF16)
        v_row[there, :] = v_ref[here, :].astype(BF16)

    tall = max(QUERY_BLOCK, rows)

    def query_step(first, width):
        queries = q_row[pl.ds(first, tall), :]
        places = first + lax.broadcasted_iota(jnp.int32, (tall, 1), 0)
        keys_at = lax.broadcasted_iota(jnp.int32, (tall, width), 1)
        allowed = (keys_at <= places) & (keys_at >= document_start(places, info_ref))
        results = []
        logs = []
        for head in range(2):
            scores = dot_nt(only_head(queries, head), k_row[:width, :])
            scores = jnp.where(allowed, scores, NEGATIVE)
            highest = jnp.max(scores, axis=1, keepdims=True)
            weights = jnp.exp(scores - highest)
            total = jnp.sum(weights, axis=1, keepdims=True)
            results.append(dot_nn(weights.astype(BF16), v_row[:width, :]) / total)
            logs.append(highest + jnp.log(total))
        first_head = head_lanes((tall, PAIR), 0)
        present = (places < info_ref[3]).astype(F32)
        merged = (jnp.where(first_head, results[0], results[1]) * present).astype(BF16)
        log_ref[pl.ds(first, tall), :] = jnp.where(first_head, logs[0], logs[1])
        return merged

    def put(merged, first_block):
        for part in range(tall // rows):
            here = relative_place(first_block + part, info_ref, blocks, rows)
            out_ref[here, :] = merged[part * rows : (part + 1) * rows]

    steps = length // tall
    if steps <= UNROLLED:
        for step in range(steps):
            put(query_step(step * tall, (step + 1) * tall), step * (tall // rows))
    else:

        @pl.loop(0, steps)
        def _(step):
            put(query_step(pl.multiple_of(step * tall, tall), length), step * (tall // rows))


def attend(info, projected, cosine, sine, blocks):
    length, width = projected.shape
    pairs = width // 3 // PAIR
    whole = lambda kind: pl.BlockSpec((length, PAIR), lambda p, _: (0, kind * pairs + p))
    table = pl.BlockSpec((length, PAIR), lambda p, _: (0, 0))
    shape = lambda kind: jax.ShapeDtypeStruct((length, pairs * PAIR), kind)
    return pl.pallas_call(
        functools.partial(attend_kernel, blocks),
        grid_spec=pltpu.PrefetchScalarGridSpec(
            num_scalar_prefetch=1,
            grid=(pairs,),
            in_specs=[whole(0), whole(1), whole(2), table, table],
            out_specs=[whole(0)] * 5,
        ),
        out_shape=[shape(BF16), shape(BF16), shape(BF16), shape(BF16), shape(F32)],
        compiler_params=pltpu.CompilerParams(vmem_limit_bytes=48 * 2**20),
        cost_estimate=pl.CostEstimate(
            flops=8 * pairs * length * length * PAIR // 2,
            bytes_accessed=6 * length * width,
            transcendentals=pairs * length * length,
        ),
        name="attend",
    )(info, projected, projected, projected, cosine, sine)


def attend_back_kernel(
    blocks,
    info_ref,
    q_row,
    k_row,
    v_row,
    log_ref,
    out_ref,
    grad_ref,
    cos_ref,
    sin_ref,
    back_ref,
    g_row,
    q_sum,
    k_sum,
    v_sum,
    log_flat,
    inner_flat,
):
    length = q_row.shape[0]
    rows = length // blocks
    score_scale = HEAD_DIM ** (-0.5)
    kind = pl.program_id(1)
    tall = max(QUERY_BLOCK, rows)

    @pl.when(kind == 0)
    def _():
        for block in range(blocks):
            here = relative_place(block, info_ref, blocks, rows)
            there = pl.ds(block * rows, rows)
            places = block * rows + lax.broadcasted_iota(jnp.int32, (rows, 1), 0)
            present = (places < info_ref[3]).astype(F32)
            grads = grad_ref[here, :].astype(F32) * present
            g_row[there, :] = grads.astype(BF16)
            inner = (grads * out_ref[here, :].astype(F32)).T
            for head in range(2):
                span = slice(head * HEAD_DIM, (head + 1) * HEAD_DIM)
                inner_flat[head : head + 1, there] = jnp.sum(inner[span], axis=0, keepdims=True)
            logs = log_ref[there, :].T
            for head in range(2):
                log_flat[head : head + 1, there] = logs[head * HEAD_DIM : head * HEAD_DIM + 1]
        q_sum[...] = jnp.zeros_like(q_sum)

        def key_step(first, from_query):
            width = length - from_query
            span = slice(from_query, length)
            keys = k_row[pl.ds(first, tall), :]
            values = v_row[pl.ds(first, tall), :]
            keys_at = first + lax.broadcasted_iota(jnp.int32, (tall, 1), 0)
            places = from_query + lax.broadcasted_iota(jnp.int32, (1, width), 1)
            allowed = (keys_at <= places) & (keys_at >= document_start(places, info_ref))
            queries, grads = q_row[span, :], g_row[span, :]
            k_parts = []
            v_parts = []
            for head in range(2):
                keys_head = only_head(keys, head)
                scores = dot_nt(keys_head, queries)
                raised = jnp.exp(scores - log_flat[head : head + 1, span])
                weights = jnp.where(allowed, raised, 0.0)
                grad_weights = dot_nt(only_head(values, head), grads)
                grad_scores = weights * (grad_weights - inner_flat[head : head + 1, span])
                grad_scores = grad_scores.astype(BF16)
                v_parts.append(dot_nn(weights.astype(BF16), grads))
                k_parts.append(dot_nn(grad_scores, queries))
                q_sum[span, :] += dot_tn(grad_scores, keys_head)
            first_head = head_lanes((tall, PAIR), 0)
            k_sum[pl.ds(first, tall), :] = jnp.where(first_head, k_parts[0], k_parts[1])
            v_sum[pl.ds(first, tall), :] = jnp.where(first_head, v_parts[0], v_parts[1])

        steps = length // tall
        if steps <= UNROLLED:
            for step in range(steps):
                key_step(step * tall, step * tall)
        else:

            @pl.loop(0, steps)
            def _(step):
                key_step(pl.multiple_of(step * tall, tall), 0)

    def give(source, turned, scale):
        for block in range(blocks):
            here = relative_place(block, info_ref, blocks, rows)
            grads = source[pl.ds(block * rows, rows), :] * scale
            if turned:
                grads = grads * cos_ref[here, :] - swap_halves(grads) * sin_ref[here, :]
            back_ref[here, :] = grads.astype(BF16)

    pl.when(kind == 0)(lambda: give(q_sum, True, score_scale))
    pl.when(kind == 1)(lambda: give(k_sum, True, 1.0))
    pl.when(kind == 2)(lambda: give(v_sum, False, 1.0))


def attend_back(info, q_row, k_row, v_row, logs, attended, grads, cosine, sine, blocks):
    length, width = q_row.shape
    pairs = width // PAIR
    one = pl.BlockSpec((length, PAIR), lambda p, c, _: (0, p))
    table = pl.BlockSpec((length, PAIR), lambda p, c, _: (0, 0))
    return pl.pallas_call(
        functools.partial(attend_back_kernel, blocks),
        grid_spec=pltpu.PrefetchScalarGridSpec(
            num_scalar_prefetch=1,
            grid=(pairs, 3),
            in_specs=[one] * 6 + [table] * 2,
            out_specs=pl.BlockSpec((length, PAIR), lambda p, c, _: (0, c * pairs + p)),
            scratch_shapes=[
                pltpu.VMEM((length, PAIR), BF16),
                pltpu.VMEM((length, PAIR), F32),
                pltpu.VMEM((length, PAIR), F32),
                pltpu.VMEM((length, PAIR), F32),
                pltpu.VMEM((8, length), F32),
                pltpu.VMEM((8, length), F32),
            ],
        ),
        out_shape=jax.ShapeDtypeStruct((length, 3 * width), BF16),
        compiler_params=pltpu.CompilerParams(vmem_limit_bytes=48 * 2**20),
        cost_estimate=pl.CostEstimate(
            flops=20 * pairs * length * length * PAIR // 2,
            bytes_accessed=20 * length * width,
            transcendentals=pairs * length * length,
        ),
        name="attend_back",
    )(info, q_row, k_row, v_row, logs, attended, grads, cosine, sine)


def whole_pairs(values, kinds):
    own = values.shape[1] // kinds
    if own % PAIR == 0:
        return values
    values = jnp.pad(values.reshape(-1, kinds, own), ((0, 0), (0, 0), (0, PAIR - own % PAIR)))
    return values.reshape(values.shape[0], -1)


def own_heads(values, kinds, own):
    return values.reshape(values.shape[0], kinds, -1)[:, :, :own].reshape(values.shape[0], -1)


def rms_unit(values):
    factor = lax.rsqrt(jnp.mean(values * values, axis=-1, keepdims=True) + EPSILON)
    return (values * factor, factor)


def norm_back(grad_normed, unit_rows, factor, gain_row):
    scaled_grad = grad_normed * gain_row
    inner_mean = jnp.mean(scaled_grad * unit_rows, axis=-1, keepdims=True)
    return (
        factor * (scaled_grad - unit_rows * inner_mean),
        jnp.sum(grad_normed * unit_rows, axis=0),
    )


def row_layout(lengths, places):
    ends = [jnp.sum(lengths[: i + 1]) for i in range(lengths.shape[0])]
    begins = jnp.zeros_like(places)
    for end in ends:
        begins = jnp.where(places >= end, end, begins)
    return ends, places - begins


def rope_tables(within):
    half = HEAD_DIM // 2
    steps_up = jnp.arange(half, dtype=F32)
    frequency = ROPE_BASE ** (-2.0 * steps_up / HEAD_DIM)
    angles = within.astype(F32)[:, None] * frequency[None, :]
    cosine, sine = jnp.cos(angles), jnp.sin(angles)
    return (
        jnp.concatenate([cosine] * 4, axis=1),
        jnp.concatenate([-sine, sine, -sine, sine], axis=1),
    )


def body(
    tokens, doc_lengths, weight_qkv, weight_out, weight_gate_up, weight_down, norm_gains, cotangent
):
    sizes = [(axis, lax.axis_size(axis)) for axis in ("dp", "blk", "tensor")]
    size_dp, size_blk, size_tensor = (size for _, size in sizes)
    group = size_blk * size_tensor
    local_rows = tokens.shape[1]
    lengths = doc_lengths[0]

    me = (lax.axis_index("blk") * size_tensor + lax.axis_index("tensor")).astype(jnp.int32)
    order = jnp.array([*range(0, group, 2), *range(1, group, 2)], jnp.int32)
    places = (lax.bitwise_xor(order, me)[:, None] * local_rows) + jnp.arange(
        local_rows, dtype=jnp.int32
    )[None, :]
    ends, within = row_layout(lengths, places.reshape(-1))
    info = jnp.stack([me] + ends).astype(jnp.int32)
    cosine, sine = rope_tables(within)

    kinds = [weight_qkv, weight_out[:, None, :]]
    if size_blk == 2:
        sides = [jnp.concatenate(side, axis=1) for side in zip(*(split_columns(k, 2) for k in kinds))]
        full_attention = named("attention_gather", gather_rows, jnp.concatenate(sides, axis=1))
        half = full_attention.shape[1] // 2
        cut = half - split_columns(kinds[1], 2).shape[2]
        own, sent = own_then_other([full_attention[:, :half], full_attention[:, half:]])
        full_qkv = named("qkv_join", join_rows, own[:, :cut], sent[:, :cut], size_dp)
        full_out = named("out_join", join_rows, own[:, cut:], sent[:, cut:], size_dp)
    else:
        held_attention = named("attention_weights", swap_columns, kinds, size_blk)
        full_attention = jnp.concatenate(held_attention, axis=1)
        full_attention = named("attention_gather", gather_rows, full_attention)
        cut = held_attention[0].shape[1]
        full_qkv, full_out = full_attention[:, :cut], full_attention[:, cut:]
    held_gate_up, held_down = named(
        "feed_weights",
        swap_columns,
        [weight_gate_up, weight_down[:, None, :]],
        size_blk,
    )
    gain_pair = named("gain_gather", gather_small, norm_gains, sizes)
    gain_first, gain_second = gain_pair[0], gain_pair[1]

    inputs = tokens[0].astype(F32)
    unit_first, factor_first = rms_unit(inputs)
    rows_first = (unit_first * gain_first).astype(BF16)
    rows_first, held_gate_up, held_down = together(rows_first, held_gate_up, held_down)
    normed_first, last_first = named("first_spread", spread, rows_first, PLANE, group)
    full_gate_up = named(
        "gate_up_gather", gather_rows, held_gate_up, full_attention, last_first
    )
    projected = dot_nn(normed_first, full_qkv)
    features = full_out.shape[1]
    attended, q_row, k_row, v_row, logs = attend(
        info, whole_pairs(projected, 3), cosine, sine, group
    )
    attended_here = own_heads(attended, 1, features)
    branch, _ = named(
        "branch_collect", collect, attended_here, full_out, dot_nt, PLANE, group
    )
    middle = inputs + branch
    unit_second, factor_second = rms_unit(middle)
    normed_second, _ = named("second_spread", spread, (unit_second * gain_second).astype(BF16), PLANE, group)
    hidden_here = full_gate_up.shape[1] // 2
    grad_output = cotangent[0].astype(F32)
    last_rows = cotangent[0]
    if normed_second.shape[0] > LONG_ROW:
        last_rows = after(last_rows, normed_second)
    grad_feed, _ = named("cotangent_spread", spread, last_rows, PLANE, group)
    full_down = named(
        "down_gather", gather_rows, held_down, full_gate_up, normed_second, grad_feed
    )
    gate = dot_nn(normed_second, full_gate_up[:, :hidden_here])
    up = dot_nn(normed_second, full_gate_up[:, hidden_here:])
    sigmoid_gate = jax.nn.sigmoid(gate)
    activated = gate * sigmoid_gate
    hidden = (activated * up).astype(BF16)
    grad_down = dot_tn(grad_feed, hidden).astype(BF16)
    wide = full_down.shape[1]
    full_down = after(full_down, grad_down)
    down_sum = named("down_back", sum_rows, after(grad_down, full_down))
    grad_hidden = dot_nn(grad_feed, full_down)
    silu_slope = sigmoid_gate * (1.0 + gate * (1.0 - sigmoid_gate))
    grad_gates = jnp.concatenate(
        [
            (grad_hidden * up * silu_slope).astype(BF16),
            (grad_hidden * activated).astype(BF16),
        ],
        axis=1,
    )
    grad_gate_up = dot_tn(normed_second, grad_gates).astype(BF16)
    grad_normed_second, last_second = named(
        "second_grad_collect", collect, grad_gates, full_gate_up, dot_nt, PLANE, group
    )
    grad_gate_up = after(grad_gate_up, down_sum, *last_second)
    gate_up_sum = named("gate_up_back", sum_rows, grad_gate_up)
    grad_middle_norm, sum_second = norm_back(
        grad_normed_second, unit_second, factor_second, gain_second
    )
    grad_middle = grad_output + grad_middle_norm
    grad_branch, _ = named("branch_grad_spread", spread, grad_middle.astype(BF16), PLANE, group)
    [total_down] = named(
        "down_return", return_columns, after(down_sum, grad_branch), size_blk, [1], wide
    )
    grad_out = dot_tn(grad_branch, attended_here).astype(BF16)
    grad_attended = dot_nn(grad_branch, full_out).astype(BF16)
    if size_blk == 2:
        out_parts = named("out_trade", trade_rows, grad_out, size_dp)
    grad_projected = attend_back(
        info,
        q_row,
        k_row,
        v_row,
        logs,
        attended,
        whole_pairs(grad_attended, 1),
        cosine,
        sine,
        group,
    )
    grad_projected = own_heads(grad_projected, 3, features)
    if size_blk == 2:
        grad_projected, *out_parts = together(grad_projected, *out_parts)
        grad_qkv = dot_tn(normed_first, grad_projected).astype(BF16)
        qkv_parts = named("qkv_trade", trade_rows, grad_qkv, size_dp)
        parts = [qkv_parts[0], out_parts[0], qkv_parts[1], out_parts[1]]
    else:
        parts = [dot_tn(normed_first, grad_projected).astype(BF16), grad_out]
    grad_normed_first, last_grad = named(
        "first_grad_collect", collect, grad_projected, full_qkv, dot_nt, PLANE, group
    )
    both = after(jnp.concatenate(parts, axis=1), gate_up_sum, *last_grad)
    both_sum = named("attention_back", sum_rows, both)
    with jax.named_scope("feed_collect"):
        feed_hidden = after(hidden, *last_second)
        feed_out, _ = collect(
            feed_hidden, full_down, dot_nt, PLANE, group, begin=last_grad
        )
    outcome = (middle + feed_out).astype(BF16)
    grad_input_norm, sum_first = norm_back(grad_normed_first, unit_first, factor_first, gain_first)
    grad_input = grad_middle + grad_input_norm
    gain_sums = named("gain_scatter", scatter_small, jnp.stack([sum_first, sum_second]), sizes)
    [total_gate_up] = named(
        "gate_up_return", return_columns, gate_up_sum, size_blk, [2], wide
    )
    both_sum = after(both_sum, total_gate_up, total_down, outcome, grad_input, gain_sums)
    if size_blk == 2:
        half = both_sum.shape[1] // 2
        summed = both_sum.astype(F32)
        parted = own_then_other([summed[:, :half], summed[:, half:]])
        total_qkv, total_out = join_columns(parted, [3, 1], features)
    else:
        total_qkv, total_out = return_columns(both_sum, size_blk, [3, 1], features)
    return (
        outcome[None],
        grad_input[None],
        total_qkv,
        total_out[:, 0],
        total_gate_up,
        total_down[:, 0],
        gain_sums,
    )


def solution(mesh):
    return jax.shard_map(
        body,
        mesh=mesh,
        in_specs=(
            P("dp", ("blk", "tensor"), None),
            P("dp", None),
            P(("dp", "blk"), None, "tensor"),
            P(("dp", "blk"), "tensor"),
            P(("dp", "blk"), None, "tensor"),
            P(("dp", "blk"), "tensor"),
            P(None, ("dp", "blk", "tensor")),
            P("dp", ("blk", "tensor"), None),
        ),
        out_specs=(
            P("dp", ("blk", "tensor"), None),
            P("dp", ("blk", "tensor"), None),
            P(("dp", "blk"), None, "tensor"),
            P(("dp", "blk"), "tensor"),
            P(("dp", "blk"), None, "tensor"),
            P(("dp", "blk"), "tensor"),
            P(None, ("dp", "blk", "tensor")),
        ),
        check_vma=False,
    )
```
